256 devices in a mesh: rowblk: 4 (over x), colblk: 32 (over y, z), rep: 2 (over core).
Axes of the slice: x: 4, y: 4, z: 8, core: 2. Of those that a mesh axis runs over, the one named last changes fastest.
Arguments:
- tile_values: float32 [8192, 256, 256], P(('rowblk', 'colblk', 'rep')), as said below
- tile_rowpos: int32 [8192], P(('rowblk', 'colblk', 'rep')), may hold values from 0 to 63
- tile_owner: int32 [8192, 1], P(('rowblk', 'colblk', 'rep')), may hold values from 0 to 31; in each aligned block of 32 rows (0 to 31, 32 to 63, ...) at most 2 rows name the same one
- tile_colpos: int32 [8192], P(('rowblk', 'colblk', 'rep')), may hold values from 0 to 7
- cost_vector: float32 [65536], P('colblk'), may hold values from -6 to 6
- upper_bound: float32 [65536], P('colblk'), may hold values from 0.5 to 2
- primal_start: float32 [65536], P('colblk'), may hold values from 0 to 0.5
- row_limits: float32 [65536], P('rowblk'), may hold values from 0.5 to 4
- sense_flags: int32 [65536], P('rowblk'), may hold values 0 or 1
- dual_start: float32 [65536], P('rowblk'), may hold values from 0 to 1
- step_sizes: float32 [2], replicated, may hold values from 0.005 to 0.05
Outputs:
- primal: float32 [65536], P('colblk')
- dual_values: float32 [65536], P('rowblk')
The draws below stay inside these ranges and needn't reach their ends.
Inputs may be any that keep to these rules, and one draw needn't show every extreme that they name: `tile_owner`: among the 32 tiles of one device (aligned blocks of 32 entries), no value appears more than 2 times, and some value appears exactly 2 times. `tile_values`: entries are finite.
All inputs are finite; a program needn't handle non-finite values. No bound on the sum of `sense_flags` on one device may be relied on, other than what follows from the above.
Results may differ from the reference program's by a relative error of at most 0.0003.
Values sent between devices are 32-bit elements; how exact they have to be, the bound alone decides.
No kernel may reach another device: no remote copies, remote signals or barrier semaphores. Data moves between devices by JAX's collectives and lax.ppermute only.
A program may use at most 128 MiB of HBM per device.

```python
import math
import jax
import jax.numpy as jnp
import numpy as np
from jax import lax

TILE = 256
TPD = 32
RB_DEV = 64
CB_DEV = 8
PASSES = 2
ITERS = 2
CAP = 2
TILES = 8192
ROWS = 65536
COLS = 65536
N_ROWBLK = 4
N_COLBLK = 32


def draw_tile_values(key, part):
    key = jax.random.fold_in(key, 11)
    first, second, third, fourth, fifth = jax.random.split(key, 5)
    base = jnp.clip(jax.random.normal(first, (TILES, TILE, TILE), jnp.float32), -6.0, 6.0)
    spread_limit = 1.15
    faint_count = max(1, TILE // 16)
    faint_rows = jax.random.permutation(fourth, TILE) < faint_count
    faint_cols = jax.random.permutation(fifth, TILE) < faint_count
    row_damp = jnp.where(faint_rows, 0.001, 1.0).astype(jnp.float32)
    col_damp = jnp.where(faint_cols, 0.001, 1.0).astype(jnp.float32)
    row_factor = jnp.exp(jax.random.uniform(second, (TILES, TILE, 1), jnp.float32, -spread_limit, spread_limit))
    col_factor = jnp.exp(jax.random.uniform(third, (TILES, 1, TILE), jnp.float32, -spread_limit, spread_limit))
    row_factor = row_factor * row_damp[None, :, None]
    col_factor = col_factor * col_damp[None, None, :]
    return base * row_factor * col_factor


def set_ends(array, own_key, low, largest):
    place = [jax.random.randint(jax.random.fold_in(own_key, axis), (), 0, length) for axis, length in enumerate(array.shape)]
    widest = array.shape.index(max(array.shape))
    neighbour = place[:widest] + [(place[widest] + 1) % array.shape[widest]] + place[widest + 1:]
    return array.at[tuple(place)].set(low).at[tuple(neighbour)].set(largest)


def block_levels(key, shape, cuts, smallest, largest):
    gain = 1.0
    for dim, parts in cuts:
        draws = jax.random.uniform(jax.random.fold_in(jax.random.fold_in(key, 6), dim), (parts,), jnp.float32, smallest / len(cuts), largest / len(cuts))
        gain = gain * jnp.repeat(jnp.exp(draws), shape[dim] // parts).reshape((-1,) + (1,) * (len(shape) - 1 - dim))
    return gain


def assign_block(rng, own, number, rows, amount, top, limit, skew):
    ranking = jax.random.permutation(rng, amount)
    heavy_load, usual = load_shares(amount, rows * top, limit, skew, True), load_shares(amount, rows * top, limit, skew, False)
    places = jnp.arange(amount)

    def named(lengths, rotation):
        used = int((lengths > 0).sum())
        fixed = max(1, used // 4)
        passed = fixed + (places - fixed + rotation * (used - fixed)) % max(1, amount - fixed)
        return jnp.zeros((amount,), jnp.int32).at[ranking[jnp.where(places < fixed, places, passed)]].set(jnp.asarray(lengths, jnp.int32))

    lengths = jnp.where(number % 4 == 0, named(heavy_load, number // 4), named(usual, number - number // 4 - 1))
    mixed = jax.random.permutation(jax.random.fold_in(own, 3), amount)
    donor, receiver = mixed[0:amount // 2 * 2:2], mixed[1:amount // 2 * 2:2]
    slack = jnp.minimum(lengths[donor] - 1, limit - lengths[receiver]) // 2
    slack = jnp.where((donor == ranking[0]) | (receiver == ranking[0]) | (lengths[receiver] == 0), 0, jnp.maximum(slack, 0))
    passed = jax.random.randint(jax.random.fold_in(own, 4), (amount // 2,), 0, 1 << 20) % (slack + 1)
    lengths = lengths.at[donor].add(-passed).at[receiver].add(passed)
    items = jnp.searchsorted(jnp.cumsum(lengths), jnp.arange(rows * top), side="right").astype(jnp.int32)
    grid = items.reshape(top, rows).T
    grid = grid[jax.random.permutation(jax.random.fold_in(own, 1), rows)]
    rotation = jax.random.randint(jax.random.fold_in(own, 2), (rows, 1), 0, top)
    return jnp.take_along_axis(grid, (jnp.arange(top)[None, :] + rotation) % top, axis=1)


def load_shares(number_of, total, most, lean, full):
    weights = [(1 << 20) // math.isqrt(rank ** lean) + 1 for rank in range(1, number_of + 1)]
    largest = most if full else min(most, max(-(-total // number_of), total * weights[0] // sum(weights)))
    least = 1 if total - largest >= number_of - 1 else 0
    holding, surplus = [largest] + [least] * (number_of - 1), total - largest - least * (number_of - 1)
    while surplus > 0:
        candidates = [i for i in range(1, number_of) if holding[i] < largest] or [i for i in range(1, number_of) if holding[i] < most]
        whole, budget = sum([weights[i] for i in candidates]), surplus
        for i in candidates:
            extra = min(most - holding[i], max(1, budget * weights[i] // whole), surplus)
            holding[i] = holding[i] + extra
            surplus = surplus - extra
    return np.array(holding)


def normal_values(key, dims, width, reach, cuts=(), held_as=jnp.bfloat16):
    array = jax.random.normal(key, dims, jnp.float32) * width
    if len(cuts) > 0:
        array = block_levels(key, dims, cuts, -0.22, 0.18) * array
    return jnp.clip(array, min=-reach, max=reach).astype(held_as)


def setup_inputs(seed: int = 0) -> dict:
    keys = jax.random.split(jax.random.key(seed), 12)
    tile_values = draw_tile_values(jax.random.fold_in(keys[11], 71), 0)
    tile_rowpos = set_ends(jax.random.randint(keys[1], (TILES,), 0, RB_DEV), jax.random.fold_in(keys[1], 1), 0, RB_DEV - 1).astype(jnp.int32)
    tile_owner_keys = jax.random.split(jax.random.fold_in(keys[2], 1), TILES // TPD)
    tile_owner_turns = jax.random.permutation(jax.random.fold_in(keys[2], 3), TILES // TPD)
    tile_owner = jax.vmap(lambda own, number: assign_block(jax.random.fold_in(keys[2], 2), own, number, TPD, N_COLBLK, 1, CAP, 2))(tile_owner_keys, tile_owner_turns).reshape((TILES, 1))
    tile_colpos = set_ends(jax.random.randint(keys[3], (TILES,), 0, CB_DEV), jax.random.fold_in(keys[3], 1), 0, CB_DEV - 1).astype(jnp.int32)
    cost_vector = normal_values(keys[4], (COLS,), 1.0, 6.0, ((0, 32),), jnp.float32)
    upper_bound = jnp.clip(jnp.exp(math.log(2.0) - 1.3862944 * jax.random.uniform(keys[5], (COLS,), jnp.float32) ** block_levels(keys[5], (COLS,), ((0, 32),), -0.2, 0.2)), 0.5, 2.0)
    primal_start = jnp.clip(0.5 * jax.random.uniform(keys[6], (COLS,), jnp.float32) ** block_levels(keys[6], (COLS,), ((0, 32),), -0.2, 0.2), 0.0, 0.5)
    row_limits = jnp.clip(jnp.exp(math.log(4.0) - 2.0794415 * jax.random.uniform(keys[7], (ROWS,), jnp.float32) ** block_levels(keys[7], (ROWS,), ((0, 4),), -0.2, 0.2)), 0.5, 4.0)
    sense_flags = set_ends((jax.random.randint(keys[8], (ROWS,), 0, 4) < 3).astype(jnp.int32), jax.random.fold_in(keys[8], 1), 0, 1)
    dual_start = jnp.clip(1.0 * jax.random.uniform(keys[9], (ROWS,), jnp.float32) ** block_levels(keys[9], (ROWS,), ((0, 4),), -0.2, 0.2), 0.0, 1.0)
    step_sizes = jnp.clip(jnp.exp(jax.random.uniform(keys[10], (2,), jnp.float32, math.log(0.005), math.log(0.05))), 0.005, 0.05)
    return {"tile_values": tile_values, "tile_rowpos": tile_rowpos, "tile_owner": tile_owner, "tile_colpos": tile_colpos, "cost_vector": cost_vector, "upper_bound": upper_bound, "primal_start": primal_start, "row_limits": row_limits, "sense_flags": sense_flags, "dual_start": dual_start, "step_sizes": step_sizes}


FLOOR = 0.5
EXACT = lax.Precision.HIGHEST

def tile_blocks(tile_rowpos, tile_owner, tile_colpos):
    count = tile_rowpos.shape[0]
    per_rowblk = count // N_ROWBLK
    order = jnp.arange(count, dtype=jnp.int32)
    row_block = order // per_rowblk * RB_DEV + tile_rowpos
    col_block = tile_owner[:, 0] * CB_DEV + tile_colpos
    return (row_block.astype(jnp.int32), col_block.astype(jnp.int32))

def scaled_square(square, row_block, col_block, row_scale, col_scale):
    row_part = lax.dynamic_slice_in_dim(row_scale, row_block * TILE, TILE)
    col_part = lax.dynamic_slice_in_dim(col_scale, col_block * TILE, TILE)
    return row_part[:, None] * square * col_part[None, :]

def maxima(tile_values, row_blocks, col_blocks, row_scale, col_scale):

    def advance(running, element):
        row_peak, col_peak = running
        square, row_block, col_block = element
        magnitude = jnp.abs(scaled_square(square, row_block, col_block, row_scale, col_scale))
        row_offset = row_block * TILE
        col_offset = col_block * TILE
        current = lax.dynamic_slice_in_dim(row_peak, row_offset, TILE)
        row_peak = lax.dynamic_update_slice_in_dim(row_peak, jnp.maximum(current, magnitude.max(axis=1)), row_offset, 0)
        current = lax.dynamic_slice_in_dim(col_peak, col_offset, TILE)
        col_peak = lax.dynamic_update_slice_in_dim(col_peak, jnp.maximum(current, magnitude.max(axis=0)), col_offset, 0)
        return ((row_peak, col_peak), None)
    start_state = (jnp.zeros((ROWS,), jnp.float32), jnp.zeros((COLS,), jnp.float32))
    result, _ = lax.scan(advance, start_state, (tile_values, row_blocks, col_blocks))
    return result

def apply_forward(tile_values, row_blocks, col_blocks, row_scale, col_scale, vector):

    def advance(summed, element):
        square, row_block, col_block = element
        scaled = scaled_square(square, row_block, col_block, row_scale, col_scale)
        segment = lax.dynamic_slice_in_dim(vector, col_block * TILE, TILE)
        offset = row_block * TILE
        current = lax.dynamic_slice_in_dim(summed, offset, TILE)
        summed = lax.dynamic_update_slice_in_dim(summed, current + jnp.dot(scaled, segment, precision=EXACT), offset, 0)
        return (summed, None)
    summed, _ = lax.scan(advance, jnp.zeros((ROWS,), jnp.float32), (tile_values, row_blocks, col_blocks))
    return summed

def apply_transpose(tile_values, row_blocks, col_blocks, row_scale, col_scale, vector):

    def advance(summed, element):
        square, row_block, col_block = element
        scaled = scaled_square(square, row_block, col_block, row_scale, col_scale)
        segment = lax.dynamic_slice_in_dim(vector, row_block * TILE, TILE)
        offset = col_block * TILE
        current = lax.dynamic_slice_in_dim(summed, offset, TILE)
        summed = lax.dynamic_update_slice_in_dim(summed, current + jnp.dot(segment, scaled, precision=EXACT), offset, 0)
        return (summed, None)
    summed, _ = lax.scan(advance, jnp.zeros((COLS,), jnp.float32), (tile_values, row_blocks, col_blocks))
    return summed

def reference(tile_values, tile_rowpos, tile_owner, tile_colpos, cost_vector, upper_bound, primal_start, row_limits, sense_flags, dual_start, step_sizes):
    row_blocks, col_blocks = tile_blocks(tile_rowpos, tile_owner, tile_colpos)
    row_scale = jnp.ones((ROWS,), jnp.float32)
    col_scale = jnp.ones((COLS,), jnp.float32)
    for sweep_index in range(PASSES):
        row_peak, col_peak = maxima(tile_values, row_blocks, col_blocks, row_scale, col_scale)
        row_scale = row_scale / jnp.sqrt(jnp.maximum(row_peak, FLOOR))
        col_scale = col_scale / jnp.sqrt(jnp.maximum(col_peak, FLOOR))
    cost_scaled = col_scale * cost_vector
    upper_scaled = upper_bound / col_scale
    limit_scaled = row_scale * row_limits
    primal_now = primal_start / col_scale
    dual_now = dual_start / row_scale
    primal_step = step_sizes[0]
    dual_step = step_sizes[1]
    for repeat_index in range(ITERS):
        gradient = apply_transpose(tile_values, row_blocks, col_blocks, row_scale, col_scale, dual_now)
        primal_next = jnp.clip(primal_now - primal_step * (cost_scaled + gradient), 0.0, upper_scaled)
        image = apply_forward(tile_values, row_blocks, col_blocks, row_scale, col_scale, 2.0 * primal_next - primal_now)
        dual_next = dual_now + dual_step * (image - limit_scaled)
        dual_now = jnp.where(sense_flags == 1, jnp.maximum(dual_next, 0.0), dual_next)
        primal_now = primal_next
    return (col_scale * primal_now, row_scale * dual_now)
```

```python
import functools

import jax
import jax.numpy as jnp
from jax import lax
from jax.experimental import pallas as pl
from jax.experimental.pallas import tpu as pltpu
from jax.sharding import PartitionSpec as P

FLOOR = 0.5
CAP = 2
LANES = 128
GROUP = 4
PLANE = ("colblk", "rep")
F32 = jnp.float32
BF16 = jnp.bfloat16
VMEM_LIMIT = 40 * 1024 * 1024


def params():
    return pltpu.CompilerParams(vmem_limit_bytes=VMEM_LIMIT)


def row_of(ref, index):
    return ref[pl.ds(index, 1), :]


def both_halves(low, high):
    return jnp.concatenate([low, high], axis=1)


def peak_over_lanes(magnitude):
    folded = jnp.maximum(magnitude[:, :LANES], magnitude[:, LANES:])
    return jnp.max(folded.T, axis=0, keepdims=True)


def two_terms(vector):
    first = vector.astype(BF16).astype(F32)
    second = vector - first
    rows = lax.broadcasted_iota(jnp.int32, (16, vector.shape[1]), 0)
    stacked = jnp.where(rows == 0, first, jnp.where(rows == 1, second, 0.0))
    return stacked.astype(BF16)


def times(vector, high, low, contract):
    left = two_terms(vector)
    dims = (((1,), (contract,)), ((), ()))
    total = lax.dot_general(left, high, dims, preferred_element_type=F32)
    total = total + lax.dot_general(left, low, dims, preferred_element_type=F32)
    return jnp.sum(total, axis=0, keepdims=True)


def places(index_ref, tile, tiles):
    return (
        index_ref[tile],
        2 * index_ref[tiles + tile],
        index_ref[2 * tiles + tile],
        index_ref[3 * tiles + tile],
    )


def first_peaks_kernel(tiles, index_ref, tile_ref, out_ref):
    step = pl.program_id(0)

    @pl.when(step == 0)
    def _():
        out_ref[...] = jnp.zeros_like(out_ref)

    for u in range(GROUP):
        row, owner, slot, position = places(index_ref, step * GROUP + u, tiles)
        magnitude = jnp.abs(tile_ref[u])
        columns = jnp.max(magnitude, axis=0, keepdims=True)
        rows = peak_over_lanes(magnitude)
        place = jnp.zeros((1, LANES), F32) + position.astype(F32)
        for h in range(2):
            out_ref[pl.ds((owner + h) * 8 + slot, 1), :] = columns[:, h * LANES:(h + 1) * LANES]
            out_ref[pl.ds((owner + h) * 8 + 4 + slot, 1), :] = place
            at = row * 8 + 2 + h
            out_ref[pl.ds(at, 1), :] = jnp.maximum(
                row_of(out_ref, at), rows[:, h * LANES:(h + 1) * LANES]
            )


def second_peaks_kernel(tiles, index_ref, tile_ref, scale_ref, dual_ref, out_ref, high_ref, low_ref):
    step = pl.program_id(0)

    @pl.when(step == 0)
    def _():
        out_ref[...] = jnp.zeros_like(out_ref)

    for u in range(GROUP):
        row, owner, slot, _ = places(index_ref, step * GROUP + u, tiles)
        row_scale = [row_of(scale_ref, row * 4 + 2 + h) for h in range(2)]
        down = jnp.concatenate(
            [jnp.broadcast_to(part, (LANES, LANES)).T for part in row_scale], axis=0
        )
        col_scale = [row_of(scale_ref, (owner + h) * 4 + slot) for h in range(2)]
        square = tile_ref[u]
        scaled = jnp.concatenate(
            [(down * square[:, h * LANES:(h + 1) * LANES]) * col_scale[h] for h in range(2)], axis=1
        )
        magnitude = jnp.abs(scaled)
        columns = jnp.max(magnitude, axis=0, keepdims=True)
        rows = peak_over_lanes(magnitude)
        high = scaled.astype(BF16)
        low = (scaled - high.astype(F32)).astype(BF16)
        high_ref[u] = high
        low_ref[u] = low
        duals = both_halves(*[row_of(dual_ref, row * 2 + h) / row_scale[h] for h in range(2)])
        sums = times(duals, high, low, 0)
        for h in range(2):
            part = slice(h * LANES, (h + 1) * LANES)
            out_ref[pl.ds((owner + h) * 8 + slot, 1), :] = columns[:, part]
            out_ref[pl.ds((owner + h) * 8 + 4 + slot, 1), :] = sums[:, part]
            at = row * 8 + 2 + h
            out_ref[pl.ds(at, 1), :] = jnp.maximum(row_of(out_ref, at), rows[:, part])


def forward_kernel(tiles, index_ref, high_ref, low_ref, vector_ref, out_ref):
    step = pl.program_id(0)

    @pl.when(step == 0)
    def _():
        out_ref[...] = jnp.zeros_like(out_ref)

    for u in range(GROUP):
        row, owner, slot, _ = places(index_ref, step * GROUP + u, tiles)
        vector = both_halves(*[row_of(vector_ref, (owner + h) * 2 + slot) for h in range(2)])
        sums = times(vector, high_ref[u], low_ref[u], 1)
        for h in range(2):
            at = row * 2 + h
            out_ref[pl.ds(at, 1), :] = row_of(out_ref, at) + sums[:, h * LANES:(h + 1) * LANES]


def transposed_kernel(tiles, index_ref, high_ref, low_ref, vector_ref, out_ref):
    step = pl.program_id(0)

    @pl.when(step == 0)
    def _():
        out_ref[...] = jnp.zeros_like(out_ref)

    for u in range(GROUP):
        row, owner, slot, _ = places(index_ref, step * GROUP + u, tiles)
        vector = both_halves(*[row_of(vector_ref, row * 2 + h) for h in range(2)])
        sums = times(vector, high_ref[u], low_ref[u], 0)
        for h in range(2):
            out_ref[pl.ds((owner + h) * 2 + slot, 1), :] = sums[:, h * LANES:(h + 1) * LANES]


def every(ref, offset, stride):
    return ref[pl.ds(offset, ref.shape[0] // stride, stride=stride), :]


def gathered_by_place(table, place):
    picked = jnp.zeros_like(place)
    for q in range(table.shape[0]):
        picked = jnp.where(place == q, table[q:q + 1, :], picked)
    return picked


def peak_by_place(entries, blocks):
    out = []
    for q in range(blocks):
        best = None
        for value, place in entries:
            chosen = jnp.max(jnp.where(place == q, value, 0.0), axis=0, keepdims=True)
            best = chosen if best is None else jnp.maximum(best, chosen)
        out.append(best)
    return jnp.concatenate(out, axis=0)


def sum_by_place(entries, blocks):
    out = []
    for q in range(blocks):
        whole = None
        for value, place in entries:
            chosen = jnp.sum(jnp.where(place == q, value, 0.0), axis=0, keepdims=True)
            whole = chosen if whole is None else whole + chosen
        out.append(whole)
    return jnp.concatenate(out, axis=0)


def inverse_root(peak):
    return 1.0 / jnp.sqrt(jnp.maximum(peak, FLOOR))


def first_owner_kernel(blocks, got_ref, peak_ref, place_ref, row_ref):
    sources = got_ref.shape[0] // 8
    entries = []
    for k in range(CAP):
        place = every(got_ref, 4 + k, 8)
        place_ref[k * sources:(k + 1) * sources, :] = place
        entries.append((every(got_ref, k, 8), place))
    peak_ref[...] = peak_by_place(entries, blocks)
    for h in range(2):
        row_ref[h:h + 1, :] = inverse_root(jnp.max(every(got_ref, 2 + h, 8), axis=0, keepdims=True))


def first_scale_kernel(p0, p1, p2, p3, place_ref, row_ref, out_ref, scale_ref):
    peak = jnp.maximum(jnp.maximum(p0[...], p1[...]), jnp.maximum(p2[...], p3[...]))
    scale = inverse_root(peak)
    scale_ref[...] = scale
    sources = place_ref.shape[0] // CAP
    for k in range(CAP):
        place = place_ref[k * sources:(k + 1) * sources, :]
        out_ref[pl.ds(k, sources, stride=4), :] = gathered_by_place(scale, place)
    for h in range(2):
        out_ref[pl.ds(2 + h, sources, stride=4), :] = jnp.broadcast_to(
            row_ref[h:h + 1, :], (sources, LANES)
        )


def second_owner_kernel(blocks, got_ref, place_ref, both_ref, factor_ref):
    sources = got_ref.shape[0] // 8
    peaks, sums = [], []
    for k in range(CAP):
        place = place_ref[k * sources:(k + 1) * sources, :]
        peaks.append((every(got_ref, k, 8), place))
        sums.append((every(got_ref, 4 + k, 8), place))
    both_ref[0:blocks, :] = peak_by_place(peaks, blocks)
    both_ref[blocks:2 * blocks, :] = sum_by_place(sums, blocks)
    for h in range(2):
        factor_ref[h:h + 1, :] = inverse_root(
            jnp.max(every(got_ref, 2 + h, 8), axis=0, keepdims=True)
        )


def own_columns(ref, blocks):
    first = ref[pl.ds(0, blocks, stride=2), :]
    second = ref[pl.ds(1, blocks, stride=2), :]
    return jnp.where(lax.axis_index("rep") == 0, first, second)


def first_primal_kernel(
    b0, b1, b2, b3, place_ref, scale_ref, cost_ref, upper_ref, start_ref, step_ref,
    out_ref, state_ref,
):
    blocks = scale_ref.shape[0]
    peak = jnp.maximum(
        jnp.maximum(b0[0:blocks], b1[0:blocks]), jnp.maximum(b2[0:blocks], b3[0:blocks])
    )
    sums = (b0[blocks:] + b1[blocks:]) + (b2[blocks:] + b3[blocks:])
    root = jnp.sqrt(jnp.maximum(peak, FLOOR))
    factor = 1.0 / root
    scale = scale_ref[...] / root
    cost = scale * own_columns(cost_ref, blocks)
    upper = own_columns(upper_ref, blocks) / scale
    before = own_columns(start_ref, blocks) / scale
    after = jnp.clip(before - step_ref[0] * (cost + factor * sums), 0.0, upper)
    send = factor * (2.0 * after - before)
    for n, value in enumerate((factor, scale, cost, upper, after)):
        state_ref[n * blocks:(n + 1) * blocks, :] = value
    sources = place_ref.shape[0] // CAP
    for k in range(CAP):
        place = place_ref[k * sources:(k + 1) * sources, :]
        out_ref[pl.ds(k, sources, stride=2), :] = gathered_by_place(send, place)


def column_sum_kernel(blocks, got_ref, place_ref, out_ref):
    sources = got_ref.shape[0] // 2
    out_ref[...] = sum_by_place(
        [(every(got_ref, k, 2), place_ref[k * sources:(k + 1) * sources, :]) for k in range(CAP)],
        blocks,
    )


def second_primal_kernel(s0, s1, s2, s3, place_ref, state_ref, step_ref, out_ref, primal_ref):
    blocks = s0.shape[0]
    factor, scale, cost, upper, before = (
        state_ref[n * blocks:(n + 1) * blocks, :] for n in range(5)
    )
    sums = (s0[...] + s1[...]) + (s2[...] + s3[...])
    after = jnp.clip(before - step_ref[0] * (cost + factor * sums), 0.0, upper)
    send = factor * (2.0 * after - before)
    primal_ref[...] = scale * after
    sources = place_ref.shape[0] // CAP
    for k in range(CAP):
        place = place_ref[k * sources:(k + 1) * sources, :]
        out_ref[pl.ds(k, sources, stride=2), :] = gathered_by_place(send, place)


def own_rows(ref):
    mine = 2 * lax.axis_index("colblk") + lax.axis_index("rep")
    return ref[pl.ds(2 * mine, 2), :]


def dual_step_kernel(
    last, got_ref, scale_ref, factor_ref, limit_ref, sense_ref, dual_ref, step_ref,
    out_ref, *next_ref,
):
    sources = got_ref.shape[0] // 2
    image = jnp.concatenate(
        [jnp.sum(every(got_ref, h, 2), axis=0, keepdims=True) for h in range(2)], axis=0
    )
    factor = factor_ref[...]
    scale = scale_ref[...] * factor
    before = dual_ref[...] if last else own_rows(dual_ref) / scale
    limit = scale * own_rows(limit_ref)
    after = before + step_ref[1] * (factor * image - limit)
    after = jnp.where(own_rows(sense_ref) == 1, jnp.maximum(after, 0.0), after)
    if not last:
        next_ref[0][...] = after
    send = (scale if last else factor) * after
    for h in range(2):
        out_ref[pl.ds(h, sources, stride=2), :] = jnp.broadcast_to(
            send[h:h + 1, :], (sources, LANES)
        )


def over_tiles(kernel, index, tile_arrays, whole_arrays, out_rows, writes_tiles=False):
    tiles, size = tile_arrays[0].shape[0], tile_arrays[0].shape[1]
    tile_spec = pl.BlockSpec((GROUP, size, size), lambda i, index_ref: (i, 0, 0))
    whole = lambda shape: pl.BlockSpec(shape, lambda i, index_ref: (0, 0))
    out_shape = [jax.ShapeDtypeStruct((out_rows, LANES), F32)]
    out_specs = [whole((out_rows, LANES))]
    if writes_tiles:
        out_shape += [jax.ShapeDtypeStruct((tiles, size, size), BF16)] * 2
        out_specs += [tile_spec] * 2
    result = pl.pallas_call(
        functools.partial(kernel, tiles),
        grid_spec=pltpu.PrefetchScalarGridSpec(
            num_scalar_prefetch=1,
            grid=(tiles // GROUP,),
            in_specs=[tile_spec] * len(tile_arrays) + [whole(a.shape) for a in whole_arrays],
            out_specs=out_specs,
        ),
        out_shape=out_shape,
        compiler_params=params(),
    )(index, *tile_arrays, *whole_arrays)
    return result if writes_tiles else result[0]


def at_owner(kernel, out_rows, *arrays, scalars=None):
    specs = [pl.BlockSpec(memory_space=pltpu.VMEM) for _ in arrays]
    operands = list(arrays)
    if scalars is not None:
        specs.append(pl.BlockSpec(memory_space=pltpu.SMEM))
        operands.append(scalars)
    return pl.pallas_call(
        kernel,
        in_specs=specs,
        out_specs=[pl.BlockSpec(memory_space=pltpu.VMEM) for _ in out_rows],
        out_shape=[jax.ShapeDtypeStruct((rows, LANES), F32) for rows in out_rows],
        compiler_params=params(),
    )(*operands)


def swap(message):
    devices = lax.axis_size("colblk") * lax.axis_size("rep")
    each = message.shape[0] // devices
    sent = message.reshape(devices, each, LANES)
    got = lax.all_to_all(sent, PLANE, 0, 0, tiled=True)
    return got.reshape(message.shape)


def from_all_planes(value):
    planes = lax.axis_size("rowblk")
    return [value] + [
        lax.ppermute(value, "rowblk", [(i, i ^ m) for i in range(planes)]) for m in range(1, planes)
    ]


def on_device(
    tile_values,
    tile_rowpos,
    tile_owner,
    tile_colpos,
    cost_vector,
    upper_bound,
    primal_start,
    row_limits,
    sense_flags,
    dual_start,
    step_sizes,
):
    tiles, size = tile_values.shape[0], tile_values.shape[1]
    blocks = cost_vector.shape[0] // size
    devices = lax.axis_size("colblk") * lax.axis_size("rep")
    owners = tile_owner[:, 0]
    order = jnp.arange(tiles, dtype=jnp.int32)
    earlier = (owners[:, None] == owners[None, :]) & (order[None, :] < order[:, None])
    slots = jnp.sum(earlier.astype(jnp.int32), axis=1)
    index = jnp.concatenate([tile_rowpos, owners, slots, tile_colpos])
    cost, upper, start, limits, senses, duals = (
        a.reshape(-1, LANES)
        for a in (cost_vector, upper_bound, primal_start, row_limits, sense_flags, dual_start)
    )

    got = swap(over_tiles(first_peaks_kernel, index, [tile_values], [], 8 * devices))
    peak, place, row_scale = at_owner(
        functools.partial(first_owner_kernel, blocks), [blocks, CAP * devices, 2], got
    )
    message, col_scale = at_owner(
        first_scale_kernel, [4 * devices, blocks], *from_all_planes(peak), place, row_scale
    )
    message, high, low = over_tiles(
        second_peaks_kernel, index, [tile_values], [swap(message), duals], 8 * devices, True
    )
    both, row_factor = at_owner(
        functools.partial(second_owner_kernel, blocks), [2 * blocks, 2], swap(message), place
    )
    message, state = at_owner(
        first_primal_kernel, [2 * devices, 5 * blocks], *from_all_planes(both), place, col_scale,
        cost, upper, start, scalars=step_sizes,
    )
    message = over_tiles(forward_kernel, index, [high, low], [swap(message)], 2 * devices)
    message, dual_now = at_owner(
        functools.partial(dual_step_kernel, False), [2 * devices, 2], swap(message), row_scale,
        row_factor, limits, senses, duals, scalars=step_sizes,
    )
    message = over_tiles(transposed_kernel, index, [high, low], [swap(message)], 2 * devices)
    (sums,) = at_owner(
        functools.partial(column_sum_kernel, blocks), [blocks], swap(message), place
    )
    message, primal = at_owner(
        second_primal_kernel, [2 * devices, blocks], *from_all_planes(sums), place, state,
        scalars=step_sizes,
    )
    message = over_tiles(forward_kernel, index, [high, low], [swap(message)], 2 * devices)
    (message,) = at_owner(
        functools.partial(dual_step_kernel, True), [2 * devices], swap(message), row_scale,
        row_factor, limits, senses, dual_now, scalars=step_sizes,
    )
    dual_values = swap(message).reshape(-1)
    other = lax.ppermute(primal, "rep", [(0, 1), (1, 0)])
    is_first = lax.axis_index("rep") == 0
    halves = [jnp.where(is_first, primal, other), jnp.where(is_first, other, primal)]
    return jnp.stack(halves, axis=1).reshape(-1), dual_values


def solution(mesh):
    tiled = P(("rowblk", "colblk", "rep"))
    return jax.shard_map(
        on_device,
        mesh=mesh,
        in_specs=(
            P(("rowblk", "colblk", "rep"), None, None),
            tiled,
            P(("rowblk", "colblk", "rep"), None),
            tiled,
            P("colblk"),
            P("colblk"),
            P("colblk"),
            P("rowblk"),
            P("rowblk"),
            P("rowblk"),
            P(),
        ),
        out_specs=(P("colblk"), P("rowblk")),
        check_vma=False,
    )
```

```python
import functools

import jax
import jax.numpy as jnp
from jax import lax
from jax.experimental import pallas as pl
from jax.experimental.pallas import tpu as pltpu
from jax.sharding import PartitionSpec as P

FLOOR = 0.5
CAP = 2
LANES = 128
GROUP = 4
PLANE = ("colblk", "rep")
F32 = jnp.float32
BF16 = jnp.bfloat16
VMEM_LIMIT = 40 * 1024 * 1024
FIRST_VMEM_LIMIT = 50 * 1024 * 1024
FIRST_GROUP = 4
SMALL = 2.0 ** -40
LARGE = 2.0 ** 40


def params(limit=VMEM_LIMIT):
    return pltpu.CompilerParams(vmem_limit_bytes=limit)


def row_of(ref, index):
    return ref[pl.ds(index, 1), :]


def both_halves(low, high):
    return jnp.concatenate([low, high], axis=1)


def peak_over_lanes(magnitude):
    folded = jnp.maximum(magnitude[:, :LANES], magnitude[:, LANES:])
    return jnp.max(folded.T, axis=0, keepdims=True)


def two_terms(vector):
    first = vector.astype(BF16).astype(F32)
    second = vector - first
    rows = lax.broadcasted_iota(jnp.int32, (16, vector.shape[1]), 0)
    stacked = jnp.where(rows == 0, first, jnp.where(rows == 1, second, 0.0))
    return stacked.astype(BF16)


def times(vector, high, low, contract):
    left = two_terms(vector)
    dims = (((1,), (contract,)), ((), ()))
    total = lax.dot_general(left, high, dims, preferred_element_type=F32)
    total = total + lax.dot_general(left, low, dims, preferred_element_type=F32)
    return jnp.sum(total, axis=0, keepdims=True)


def places(index_ref, tile, tiles):
    return index_ref[tile], 2 * index_ref[tiles + tile], index_ref[2 * tiles + tile]


def first_peaks_kernel(
    tiles, row_ref, owner_ref, column_ref, tile_ref, out_ref, index_ref, used_ref
):
    step = pl.program_id(0)

    @pl.when(step == 0)
    def _():
        out_ref[...] = jnp.zeros_like(out_ref)
        for owner in range(used_ref.shape[0]):
            used_ref[owner] = 0

    upper = lax.broadcasted_iota(jnp.int32, (1, LANES), 1) >= LANES // 2
    for u in range(FIRST_GROUP):
        tile = step * FIRST_GROUP + u
        row, owner, position = row_ref[tile], owner_ref[tile], column_ref[tile]
        slot = used_ref[owner]
        used_ref[owner] = slot + 1
        for n, value in enumerate((row, owner, slot)):
            index_ref[n * tiles + tile] = value
        magnitude = jnp.abs(tile_ref[u])
        columns = jnp.max(magnitude, axis=0, keepdims=True)
        rows = peak_over_lanes(magnitude)
        place = position.astype(F32)
        for h in range(2):
            part = slice(h * LANES, (h + 1) * LANES)
            base = (2 * owner + h) * 5
            out_ref[pl.ds(base + slot, 1), :] = columns[:, part]
            out_ref[pl.ds(base + 4, 1), :] = jnp.where(
                upper == (slot == 1), place, row_of(out_ref, base + 4)
            )
            at = row * 5 + 2 + h
            out_ref[pl.ds(at, 1), :] = jnp.maximum(row_of(out_ref, at), rows[:, part])


def second_peaks_kernel(tiles, index_ref, tile_ref, scale_ref, dual_ref, out_ref, high_ref, low_ref):
    step = pl.program_id(0)

    @pl.when(step == 0)
    def _():
        out_ref[...] = jnp.zeros_like(out_ref)

    for u in range(GROUP):
        row, owner, slot = places(index_ref, step * GROUP + u, tiles)
        row_scale = [row_of(scale_ref, row * 2 + h) for h in range(2)]
        down = jnp.concatenate(
            [jnp.broadcast_to(part, (LANES, LANES)).T for part in row_scale], axis=0
        )
        square = tile_ref[u]
        scaled = jnp.concatenate(
            [down * square[:, h * LANES:(h + 1) * LANES] for h in range(2)], axis=1
        )
        columns = jnp.max(jnp.abs(scaled), axis=0, keepdims=True)
        high = scaled.astype(BF16)
        low = (scaled - high.astype(F32)).astype(BF16)
        high_ref[u] = high
        low_ref[u] = low
        duals = both_halves(*[row_of(dual_ref, row * 2 + h) / row_scale[h] for h in range(2)])
        sums = times(duals * SMALL, high, low, 0)
        for h in range(2):
            part = slice(h * LANES, (h + 1) * LANES)
            at = (owner + h) * 4 + slot
            out_ref[pl.ds(at, 1), :] = columns[:, part]
            out_ref[pl.ds(at + 2, 1), :] = sums[:, part]


def forward_kernel(peaks, tiles, index_ref, high_ref, low_ref, vector_ref, out_ref):
    step = pl.program_id(0)
    rows = 4 if peaks else 2

    @pl.when(step == 0)
    def _():
        out_ref[...] = jnp.zeros_like(out_ref)

    for u in range(GROUP):
        row, owner, slot = places(index_ref, step * GROUP + u, tiles)
        high, low = high_ref[u], low_ref[u]
        at = [(owner + h) * rows + slot for h in range(2)]
        vector = both_halves(*[row_of(vector_ref, a) for a in at])
        sums = times(vector, high, low, 1)
        if peaks:
            scale = both_halves(*[row_of(vector_ref, a + 2) for a in at])
            largest = peak_over_lanes(jnp.abs((high.astype(F32) + low.astype(F32)) * scale))
        for h in range(2):
            part = slice(h * LANES, (h + 1) * LANES)
            to = row * rows + h
            out_ref[pl.ds(to, 1), :] = row_of(out_ref, to) + sums[:, part]
            if peaks:
                out_ref[pl.ds(to + 2, 1), :] = jnp.maximum(row_of(out_ref, to + 2), largest[:, part])


def transposed_kernel(tiles, index_ref, high_ref, low_ref, vector_ref, out_ref):
    step = pl.program_id(0)

    @pl.when(step == 0)
    def _():
        out_ref[...] = jnp.zeros_like(out_ref)

    for u in range(GROUP):
        row, owner, slot = places(index_ref, step * GROUP + u, tiles)
        vector = both_halves(*[row_of(vector_ref, row * 2 + h) for h in range(2)])
        sums = times(vector, high_ref[u], low_ref[u], 0)
        for h in range(2):
            out_ref[pl.ds((owner + h) * 2 + slot, 1), :] = sums[:, h * LANES:(h + 1) * LANES]


def every(ref, offset, stride):
    return ref[pl.ds(offset, ref.shape[0] // stride, stride=stride), :]


def gathered_by_place(table, place):
    picked = jnp.zeros_like(place)
    for q in range(table.shape[0]):
        picked = jnp.where(place == q, table[q:q + 1, :], picked)
    return picked


def peak_by_place(entries, blocks):
    out = []
    for q in range(blocks):
        best = None
        for value, place in entries:
            chosen = jnp.max(jnp.where(place == q, value, 0.0), axis=0, keepdims=True)
            best = chosen if best is None else jnp.maximum(best, chosen)
        out.append(best)
    return jnp.concatenate(out, axis=0)


def sum_by_place(entries, blocks):
    out = []
    for q in range(blocks):
        whole = None
        for value, place in entries:
            chosen = jnp.sum(jnp.where(place == q, value, 0.0), axis=0, keepdims=True)
            whole = chosen if whole is None else whole + chosen
        out.append(whole)
    return jnp.concatenate(out, axis=0)


def inverse_root(peak):
    return 1.0 / jnp.sqrt(jnp.maximum(peak, FLOOR))


def first_owner_kernel(blocks, got_ref, peak_ref, place_ref, row_ref, out_ref):
    sources = got_ref.shape[0] // 5
    for h in range(2):
        scale = inverse_root(jnp.max(every(got_ref, 2 + h, 5), axis=0, keepdims=True))
        row_ref[h:h + 1, :] = scale
        out_ref[pl.ds(h, sources, stride=2), :] = jnp.broadcast_to(scale, (sources, LANES))
    places_got = every(got_ref, 4, 5)
    entries = []
    for k in range(CAP):
        at = k * LANES // 2
        place = jnp.broadcast_to(places_got[:, at:at + 1], places_got.shape)
        place_ref[k * sources:(k + 1) * sources, :] = place
        entries.append((every(got_ref, k, 5), place))
    peak_ref[...] = peak_by_place(entries, blocks)


def second_owner_kernel(blocks, got_ref, place_ref, peak_ref, all_ref):
    sources = got_ref.shape[0] // 4
    peaks, sums = [], []
    for k in range(CAP):
        place = place_ref[k * sources:(k + 1) * sources, :]
        peaks.append((every(got_ref, k, 4), place))
        sums.append((every(got_ref, 2 + k, 4), place))
    all_ref[0:blocks, :] = peak_ref[...]
    all_ref[blocks:2 * blocks, :] = peak_by_place(peaks, blocks)
    all_ref[2 * blocks:3 * blocks, :] = sum_by_place(sums, blocks)


def own_columns(ref, blocks):
    first = ref[pl.ds(0, blocks, stride=2), :]
    second = ref[pl.ds(1, blocks, stride=2), :]
    return jnp.where(lax.axis_index("rep") == 0, first, second)


def first_primal_kernel(
    blocks, a0, a1, a2, a3, place_ref, cost_ref, upper_ref, start_ref, step_ref, out_ref, state_ref
):
    peaks = slice(0, 2 * blocks)
    peak = jnp.maximum(jnp.maximum(a0[peaks], a1[peaks]), jnp.maximum(a2[peaks], a3[peaks]))
    sums = (a0[2 * blocks:] + a1[2 * blocks:]) + (a2[2 * blocks:] + a3[2 * blocks:])
    first = inverse_root(peak[0:blocks])
    scale = first / jnp.sqrt(jnp.maximum(first * peak[blocks:], FLOOR))
    cost = scale * own_columns(cost_ref, blocks)
    upper = own_columns(upper_ref, blocks) / scale
    before = own_columns(start_ref, blocks) / scale
    after = jnp.clip(before - step_ref[0] * (cost + (scale * LARGE) * sums), 0.0, upper)
    send = scale * (2.0 * after - before)
    for n, value in enumerate((scale, cost, upper, after)):
        state_ref[n * blocks:(n + 1) * blocks, :] = value
    sources = place_ref.shape[0] // CAP
    for k in range(CAP):
        place = place_ref[k * sources:(k + 1) * sources, :]
        out_ref[pl.ds(k, sources, stride=4), :] = gathered_by_place(send, place)
        out_ref[pl.ds(2 + k, sources, stride=4), :] = gathered_by_place(first, place)


def column_sum_kernel(blocks, got_ref, place_ref, out_ref):
    sources = got_ref.shape[0] // 2
    out_ref[...] = sum_by_place(
        [(every(got_ref, k, 2), place_ref[k * sources:(k + 1) * sources, :]) for k in range(CAP)],
        blocks,
    )


def second_primal_kernel(s0, s1, s2, s3, place_ref, state_ref, step_ref, out_ref, primal_ref):
    blocks = s0.shape[0]
    scale, cost, upper, before = (state_ref[n * blocks:(n + 1) * blocks, :] for n in range(4))
    sums = (s0[...] + s1[...]) + (s2[...] + s3[...])
    after = jnp.clip(before - step_ref[0] * (cost + (scale * LARGE) * sums), 0.0, upper)
    send = scale * (2.0 * after - before)
    primal_ref[...] = scale * after
    sources = place_ref.shape[0] // CAP
    for k in range(CAP):
        place = place_ref[k * sources:(k + 1) * sources, :]
        out_ref[pl.ds(k, sources, stride=2), :] = gathered_by_place(send, place)


def own_rows(ref):
    mine = 2 * lax.axis_index("colblk") + lax.axis_index("rep")
    return ref[pl.ds(2 * mine, 2), :]


def total_of(got_ref, stride):
    return jnp.concatenate(
        [jnp.sum(every(got_ref, h, stride), axis=0, keepdims=True) for h in range(2)], axis=0
    )


def dual_step(before, factor, scale, image, limit_ref, sense_ref, step_ref):
    after = before + step_ref[1] * (factor * image - scale * own_rows(limit_ref))
    return jnp.where(own_rows(sense_ref) == 1, jnp.maximum(after, 0.0), after)


def to_all(out_ref, value):
    for h in range(2):
        out_ref[pl.ds(h, out_ref.shape[0] // 2, stride=2), :] = jnp.broadcast_to(
            value[h:h + 1, :], (out_ref.shape[0] // 2, LANES)
        )


def first_dual_kernel(got_ref, row_ref, limit_ref, sense_ref, dual_ref, step_ref, out_ref, state_ref):
    peak = jnp.concatenate(
        [jnp.max(every(got_ref, 2 + h, 4), axis=0, keepdims=True) for h in range(2)], axis=0
    )
    factor = inverse_root(peak)
    scale = row_ref[...] * factor
    before = own_rows(dual_ref) / scale
    after = dual_step(before, factor, scale, total_of(got_ref, 4), limit_ref, sense_ref, step_ref)
    for n, value in enumerate((factor, scale, after)):
        state_ref[2 * n:2 * n + 2, :] = value
    to_all(out_ref, (factor * SMALL) * after)


def second_dual_kernel(got_ref, state_ref, limit_ref, sense_ref, step_ref, out_ref):
    factor, scale, before = (state_ref[2 * n:2 * n + 2, :] for n in range(3))
    after = dual_step(before, factor, scale, total_of(got_ref, 2), limit_ref, sense_ref, step_ref)
    to_all(out_ref, scale * after)


def over_tiles(kernel, index, tile_arrays, whole_arrays, out_rows, writes_tiles=False):
    tiles, size = tile_arrays[0].shape[0], tile_arrays[0].shape[1]
    tile_spec = pl.BlockSpec((GROUP, size, size), lambda i, index_ref: (i, 0, 0))
    whole = lambda shape: pl.BlockSpec(shape, lambda i, index_ref: (0, 0))
    out_shape = [jax.ShapeDtypeStruct((out_rows, LANES), F32)]
    out_specs = [whole((out_rows, LANES))]
    if writes_tiles:
        out_shape += [jax.ShapeDtypeStruct((tiles, size, size), BF16)] * 2
        out_specs += [tile_spec] * 2
    result = pl.pallas_call(
        functools.partial(kernel, tiles),
        grid_spec=pltpu.PrefetchScalarGridSpec(
            num_scalar_prefetch=1,
            grid=(tiles // GROUP,),
            in_specs=[tile_spec] * len(tile_arrays) + [whole(a.shape) for a in whole_arrays],
            out_specs=out_specs,
        ),
        out_shape=out_shape,
        compiler_params=params(),
    )(index, *tile_arrays, *whole_arrays)
    return result if writes_tiles else result[0]


def at_owner(kernel, out_rows, *arrays, scalars=None):
    specs = [pl.BlockSpec(memory_space=pltpu.VMEM) for _ in arrays]
    operands = list(arrays)
    if scalars is not None:
        specs.append(pl.BlockSpec(memory_space=pltpu.SMEM))
        operands.append(scalars)
    return pl.pallas_call(
        kernel,
        in_specs=specs,
        out_specs=[pl.BlockSpec(memory_space=pltpu.VMEM) for _ in out_rows],
        out_shape=[jax.ShapeDtypeStruct((rows, LANES), F32) for rows in out_rows],
        compiler_params=params(),
    )(*operands)


def swap(message):
    devices = lax.axis_size("colblk") * lax.axis_size("rep")
    each = message.shape[0] // devices
    sent = message.reshape(devices, 1, each * LANES)
    got = lax.all_to_all(sent, PLANE, 0, 0, tiled=True)
    return got.reshape(message.shape)


def from_all_planes(value):
    planes = lax.axis_size("rowblk")
    return [value] + [
        lax.ppermute(value, "rowblk", [(i, i ^ m) for i in range(planes)]) for m in range(1, planes)
    ]


def on_device(
    tile_values,
    tile_rowpos,
    tile_owner,
    tile_colpos,
    cost_vector,
    upper_bound,
    primal_start,
    row_limits,
    sense_flags,
    dual_start,
    step_sizes,
):
    tiles, size = tile_values.shape[0], tile_values.shape[1]
    blocks = cost_vector.shape[0] // size
    devices = lax.axis_size("colblk") * lax.axis_size("rep")
    cost, upper, start, limits, senses, duals = (
        a.reshape(-1, LANES)
        for a in (cost_vector, upper_bound, primal_start, row_limits, sense_flags, dual_start)
    )

    message, index = pl.pallas_call(
        functools.partial(first_peaks_kernel, tiles),
        grid_spec=pltpu.PrefetchScalarGridSpec(
            num_scalar_prefetch=3,
            grid=(tiles // FIRST_GROUP,),
            in_specs=[pl.BlockSpec((FIRST_GROUP, size, size), lambda i, *_: (i, 0, 0))],
            out_specs=[
                pl.BlockSpec((5 * devices, LANES), lambda i, *_: (0, 0)),
                pl.BlockSpec(memory_space=pltpu.SMEM),
            ],
            scratch_shapes=[pltpu.SMEM((lax.axis_size("colblk"),), jnp.int32)],
        ),
        out_shape=[
            jax.ShapeDtypeStruct((5 * devices, LANES), F32),
            jax.ShapeDtypeStruct((3 * tiles,), jnp.int32),
        ],
        compiler_params=params(FIRST_VMEM_LIMIT),
    )(tile_rowpos, tile_owner[:, 0], tile_colpos, tile_values)
    peak, place, row_scale, message = at_owner(
        functools.partial(first_owner_kernel, blocks),
        [blocks, CAP * devices, 2, 2 * devices], swap(message),
    )
    message, high, low = over_tiles(
        second_peaks_kernel, index, [tile_values], [swap(message), duals], 4 * devices, True
    )
    (partial_sums,) = at_owner(
        functools.partial(second_owner_kernel, blocks), [3 * blocks], swap(message), place, peak
    )
    message, primal_state = at_owner(
        functools.partial(first_primal_kernel, blocks), [4 * devices, 4 * blocks],
        *from_all_planes(partial_sums), place, cost, upper, start, scalars=step_sizes,
    )
    message = over_tiles(
        functools.partial(forward_kernel, True), index, [high, low], [swap(message)], 4 * devices
    )
    message, dual_state = at_owner(
        first_dual_kernel, [2 * devices, 6], swap(message), row_scale, limits, senses, duals,
        scalars=step_sizes,
    )
    message = over_tiles(transposed_kernel, index, [high, low], [swap(message)], 2 * devices)
    (partial_sums,) = at_owner(
        functools.partial(column_sum_kernel, blocks), [blocks], swap(message), place
    )
    message, primal = at_owner(
        second_primal_kernel, [2 * devices, blocks], *from_all_planes(partial_sums), place,
        primal_state, scalars=step_sizes,
    )
    message = over_tiles(
        functools.partial(forward_kernel, False), index, [high, low], [swap(message)], 2 * devices
    )
    (message,) = at_owner(
        second_dual_kernel, [2 * devices], swap(message), dual_state, limits, senses,
        scalars=step_sizes,
    )
    dual_values = swap(message).reshape(-1)
    other = lax.ppermute(primal, "rep", [(0, 1), (1, 0)])
    is_first = lax.axis_index("rep") == 0
    halves = [jnp.where(is_first, primal, other), jnp.where(is_first, other, primal)]
    return jnp.stack(halves, axis=1).reshape(-1), dual_values


def solution(mesh):
    tiled = P(("rowblk", "colblk", "rep"))
    return jax.shard_map(
        on_device,
        mesh=mesh,
        in_specs=(
            P(("rowblk", "colblk", "rep"), None, None),
            tiled,
            P(("rowblk", "colblk", "rep"), None),
            tiled,
            P("colblk"),
            P("colblk"),
            P("colblk"),
            P("rowblk"),
            P("rowblk"),
            P("rowblk"),
            P(),
        ),
        out_specs=(P("colblk"), P("rowblk")),
        check_vma=False,
    )
```

```python
import functools

import jax
import jax.numpy as jnp
from jax import lax
from jax.experimental import pallas as pl
from jax.experimental.pallas import tpu as pltpu
from jax.sharding import PartitionSpec as P

FLOOR = 0.5
CAP = 2
LANES = 128
PLANE = ("colblk", "rep")
RING = 8
F32 = jnp.float32
BF16 = jnp.bfloat16
FIRST_VMEM_LIMIT = 43 * 1024 * 1024
TILE_VMEM_LIMIT = 34 * 1024 * 1024
OWNER_VMEM_LIMIT = 16 * 1024 * 1024
CHUNK = 2
SMALL = 2.0 ** -40
LARGE = 2.0 ** 40


def row_of(ref, index):
    return ref[pl.ds(index, 1), :]


def half(array, h):
    return array[:, h * LANES:(h + 1) * LANES]


def both_halves(low, high):
    return jnp.concatenate([low, high], axis=1)


def peak_over_lanes(magnitude):
    return jnp.max(jnp.maximum(half(magnitude, 0), half(magnitude, 1)).T, axis=0, keepdims=True)


def sum_over_lanes(products):
    return jnp.sum((half(products, 0) + half(products, 1)).T, axis=0, keepdims=True)


def down_the_rows(vector):
    parts = [jnp.broadcast_to(half(vector, h), (LANES, LANES)).T for h in range(2)]
    return jnp.concatenate(parts, axis=0)


def two_terms(vector):
    first = vector.astype(BF16).astype(F32)
    second = vector - first
    rows = lax.broadcasted_iota(jnp.int32, (16, vector.shape[1]), 0)
    stacked = jnp.where(rows == 0, first, jnp.where(rows == 1, second, 0.0))
    return stacked.astype(BF16)


def times(vector, high, low):
    left = two_terms(vector)
    total = jnp.dot(left, high, preferred_element_type=F32)
    total = total + jnp.dot(left, low, preferred_element_type=F32)
    return jnp.sum(total, axis=0, keepdims=True)


def inverse_root(peak):
    return 1.0 / jnp.sqrt(jnp.maximum(peak, FLOOR))


def places(index_ref, tile, tiles):
    row, owner, slot, position = (index_ref[n * tiles + tile] for n in range(4))
    return row, 2 * owner, slot, position


def join(out_ref, mine_ref, other_ref, parts=1):
    core = lax.axis_index("rep")
    rows = mine_ref.shape[0] // parts
    for n in range(parts):
        here = slice(n * rows, (n + 1) * rows)
        base = 2 * n * rows
        out_ref[pl.ds(pl.multiple_of(base + core * rows, 8), rows), :] = mine_ref[here, :]
        out_ref[pl.ds(pl.multiple_of(base + (1 - core) * rows, 8), rows), :] = other_ref[here, :]


def first_peaks_kernel(
    tiles, given_ref, tile_hbm, row_ref, column_ref, index_ref, tile_ref, used_ref, tile_sems
):
    def move(n):
        part = pl.ds(n * CHUNK, CHUNK)
        return pltpu.make_async_copy(tile_hbm.at[part], tile_ref.at[part], tile_sems.at[n])

    for n in range(tiles // CHUNK):
        move(n).start()
    row_ref[...] = jnp.zeros_like(row_ref)
    for owner in range(used_ref.shape[0]):
        used_ref[owner] = 0
    for tile in range(tiles):
        if tile % CHUNK == 0:
            move(tile // CHUNK).wait()
        row, owner, position = (given_ref[n * tiles + tile] for n in range(3))
        slot = used_ref[owner]
        used_ref[owner] = slot + 1
        for n, value in enumerate((row, owner, slot, position)):
            index_ref[n * tiles + tile] = value
        magnitude = jnp.abs(tile_ref[tile])
        column_ref[tile:tile + 1, :] = jnp.max(magnitude, axis=0, keepdims=True)
        rows = peak_over_lanes(magnitude)
        for h in range(2):
            at = row * 2 + h
            row_ref[pl.ds(at, 1), :] = jnp.maximum(row_of(row_ref, at), half(rows, h))


def second_peaks_kernel(
    tiles, index_ref, tile_ref, mine_ref, other_ref, column_ref, dual_ref,
    out_ref, high_ref, low_ref, scale_ref, duals,
):
    join(scale_ref, mine_ref, other_ref)
    scale_ref[...] = inverse_root(scale_ref[...])
    duals[...] = (dual_ref[...] / scale_ref[...]) * SMALL
    out_ref[...] = jnp.zeros_like(out_ref)
    upper = lax.broadcasted_iota(jnp.int32, (1, LANES), 1) >= LANES // 2
    for tile in range(tiles):
        row, owner, slot, position = places(index_ref, tile, tiles)
        down = down_the_rows(both_halves(*[row_of(scale_ref, row * 2 + h) for h in range(2)]))
        square = tile_ref[tile]
        scaled = both_halves(*[down * half(square, h) for h in range(2)])
        peaks = jnp.max(jnp.abs(scaled), axis=0, keepdims=True)
        high = scaled.astype(BF16)
        low = (scaled - high.astype(F32)).astype(BF16)
        high_ref[tile] = high
        low_ref[tile] = low
        sums = times(both_halves(*[row_of(duals, row * 2 + h) for h in range(2)]), high, low)
        before = column_ref[tile:tile + 1, :]
        for h in range(2):
            at = (owner + h) * 7
            for n, values in enumerate((before, peaks, sums)):
                out_ref[pl.ds(at + 2 * n + slot, 1), :] = half(values, h)
            out_ref[pl.ds(at + 6, 1), :] = jnp.where(
                upper == (slot == 1), position.astype(F32), row_of(out_ref, at + 6)
            )


def forward_kernel(with_peaks, tiles, index_ref, high_ref, low_ref, vector_ref, out_ref):
    each = 4 if with_peaks else 2
    part = out_ref.shape[0] // each
    out_ref[...] = jnp.zeros_like(out_ref)
    for tile in range(tiles):
        row, owner, slot, _ = places(index_ref, tile, tiles)
        at = [(owner + h) * each + slot for h in range(2)]
        entries = high_ref[tile].astype(F32) + low_ref[tile].astype(F32)
        vector = both_halves(*[row_of(vector_ref, a) for a in at])
        sums = sum_over_lanes(entries * vector)
        if with_peaks:
            scale = both_halves(*[row_of(vector_ref, a + 2) for a in at])
            peaks = peak_over_lanes(jnp.abs(entries * scale))
            start = row * 2 + jnp.where(row >= part // 2, part, 0)
        else:
            start = row * 2
        for h in range(2):
            to = start + h
            out_ref[pl.ds(to, 1), :] = row_of(out_ref, to) + half(sums, h)
            if with_peaks:
                to = to + part
                out_ref[pl.ds(to, 1), :] = jnp.maximum(row_of(out_ref, to), half(peaks, h))


def dual_step(before, factor, scale, image, limit_ref, sense_ref, step_ref):
    after = before + step_ref[1] * (factor * image - scale * limit_ref[...])
    return jnp.where(sense_ref[...] == 1, jnp.maximum(after, 0.0), after)


def transposed_kernel(
    tiles, index_ref, step_ref, high_ref, low_ref, mine_ref, other_ref, scale_ref, limit_ref,
    sense_ref, dual_ref, out_ref, state_ref, joined, send,
):
    rows = dual_ref.shape[0]
    join(joined, mine_ref, other_ref, 2)
    image = joined[0:rows, :]
    factor = inverse_root(joined[rows:2 * rows, :])
    scale = scale_ref[...] * factor
    after = dual_step(
        dual_ref[...] / scale, factor, scale, image, limit_ref, sense_ref, step_ref
    )
    for n, value in enumerate((factor, scale, after)):
        state_ref[n * rows:(n + 1) * rows, :] = value
    send[...] = (factor * SMALL) * after
    out_ref[...] = jnp.zeros_like(out_ref)
    for tile in range(tiles):
        row, owner, slot, _ = places(index_ref, tile, tiles)
        vector = both_halves(*[row_of(send, row * 2 + h) for h in range(2)])
        sums = times(vector, high_ref[tile], low_ref[tile])
        for h in range(2):
            out_ref[pl.ds((owner + h) * 2 + slot, 1), :] = half(sums, h)


def every(ref, offset, stride):
    return ref[pl.ds(offset, ref.shape[0] // stride, stride=stride), :]


def gathered_by_place(table, place):
    picked = jnp.zeros_like(place)
    for q in range(table.shape[0]):
        picked = jnp.where(place == q, table[q:q + 1, :], picked)
    return picked


def combined_by_place(entries, blocks, over, pair):
    out = []
    for q in range(blocks):
        parts = [
            over(jnp.where(place == q, value, 0.0), axis=0, keepdims=True)
            for value, place in entries
        ]
        out.append(functools.reduce(pair, parts))
    return jnp.concatenate(out, axis=0)


def peak_by_place(entries, blocks):
    return combined_by_place(entries, blocks, jnp.max, jnp.maximum)


def sum_by_place(entries, blocks):
    return combined_by_place(entries, blocks, jnp.sum, jnp.add)


def first_owner_kernel(blocks, got_ref, all_ref, place_ref):
    sources = got_ref.shape[0] // 7
    named = every(got_ref, 6, 7)
    slots = []
    for k in range(CAP):
        at = k * LANES // 2
        place = jnp.broadcast_to(named[:, at:at + 1], named.shape)
        place_ref[k * sources:(k + 1) * sources, :] = place
        slots.append(place)
    for n, by_place in enumerate((peak_by_place, peak_by_place, sum_by_place)):
        entries = [(every(got_ref, 2 * n + k, 7), slots[k]) for k in range(CAP)]
        all_ref[n * blocks:(n + 1) * blocks, :] = by_place(entries, blocks)


def own_columns(ref, blocks):
    first = ref[pl.ds(0, blocks, stride=2), :]
    second = ref[pl.ds(1, blocks, stride=2), :]
    return jnp.where(lax.axis_index("rep") == 0, first, second)


def first_primal_kernel(
    blocks, a0, a1, a2, a3, place_ref, cost_ref, upper_ref, start_ref, step_ref, out_ref, state_ref
):
    peaks = slice(0, 2 * blocks)
    peak = jnp.maximum(jnp.maximum(a0[peaks], a1[peaks]), jnp.maximum(a2[peaks], a3[peaks]))
    sums = (a0[2 * blocks:] + a1[2 * blocks:]) + (a2[2 * blocks:] + a3[2 * blocks:])
    first = inverse_root(peak[0:blocks])
    scale = first / jnp.sqrt(jnp.maximum(first * peak[blocks:], FLOOR))
    cost = scale * own_columns(cost_ref, blocks)
    upper = own_columns(upper_ref, blocks) / scale
    before = own_columns(start_ref, blocks) / scale
    after = jnp.clip(before - step_ref[0] * (cost + (scale * LARGE) * sums), 0.0, upper)
    send = scale * (2.0 * after - before)
    for n, value in enumerate((scale, cost, upper, after)):
        state_ref[n * blocks:(n + 1) * blocks, :] = value
    sources = place_ref.shape[0] // CAP
    for k in range(CAP):
        place = place_ref[k * sources:(k + 1) * sources, :]
        out_ref[pl.ds(k, sources, stride=4), :] = gathered_by_place(send, place)
        out_ref[pl.ds(2 + k, sources, stride=4), :] = gathered_by_place(first, place)


def column_sum_kernel(blocks, got_ref, place_ref, out_ref):
    sources = got_ref.shape[0] // 2
    out_ref[...] = sum_by_place(
        [(every(got_ref, k, 2), place_ref[k * sources:(k + 1) * sources, :]) for k in range(CAP)],
        blocks,
    )


def second_primal_kernel(s0, s1, s2, s3, place_ref, state_ref, step_ref, out_ref, primal_ref):
    blocks = s0.shape[0]
    scale, cost, upper, before = (state_ref[n * blocks:(n + 1) * blocks, :] for n in range(4))
    sums = (s0[...] + s1[...]) + (s2[...] + s3[...])
    after = jnp.clip(before - step_ref[0] * (cost + (scale * LARGE) * sums), 0.0, upper)
    send = scale * (2.0 * after - before)
    primal_ref[...] = scale * after
    sources = place_ref.shape[0] // CAP
    for k in range(CAP):
        place = place_ref[k * sources:(k + 1) * sources, :]
        out_ref[pl.ds(k, sources, stride=2), :] = gathered_by_place(send, place)


def last_dual_kernel(mine_ref, other_ref, state_ref, limit_ref, sense_ref, step_ref, out_ref, joined):
    rows = limit_ref.shape[0]
    join(joined, mine_ref, other_ref)
    factor, scale, before = (state_ref[n * rows:(n + 1) * rows, :] for n in range(3))
    after = dual_step(before, factor, scale, joined[...], limit_ref, sense_ref, step_ref)
    out_ref[...] = scale * after


def in_vmem():
    return pl.BlockSpec(memory_space=pltpu.VMEM)


def in_smem():
    return pl.BlockSpec(memory_space=pltpu.SMEM)


def rows_of(*counts):
    return [jax.ShapeDtypeStruct((count, LANES), F32) for count in counts]


def over_tiles(kernel, scalars, arrays, out_shape, scratch=()):
    tiles = arrays[0].shape[0]
    return pl.pallas_call(
        functools.partial(kernel, tiles),
        in_specs=[in_smem()] * len(scalars) + [in_vmem()] * len(arrays),
        out_specs=[in_vmem()] * len(out_shape),
        out_shape=out_shape,
        scratch_shapes=[pltpu.VMEM((count, LANES), F32) for count in scratch],
        compiler_params=pltpu.CompilerParams(vmem_limit_bytes=TILE_VMEM_LIMIT),
    )(*scalars, *arrays)


def first_pass(given, tile_values, row_rows, owner_count):
    tiles, size = tile_values.shape[0], tile_values.shape[1]
    return pl.pallas_call(
        functools.partial(first_peaks_kernel, tiles),
        in_specs=[in_smem(), pl.BlockSpec(memory_space=pltpu.HBM)],
        out_specs=[in_vmem(), in_vmem(), in_smem(), in_vmem()],
        out_shape=[
            jax.ShapeDtypeStruct((row_rows, LANES), F32),
            jax.ShapeDtypeStruct((tiles, size), F32),
            jax.ShapeDtypeStruct((4 * tiles,), jnp.int32),
            jax.ShapeDtypeStruct((tiles, size, size), F32),
        ],
        scratch_shapes=[
            pltpu.SMEM((owner_count,), jnp.int32), pltpu.SemaphoreType.DMA((tiles // CHUNK,)),
        ],
        compiler_params=pltpu.CompilerParams(vmem_limit_bytes=FIRST_VMEM_LIMIT),
    )(given, tile_values)


def at_owner(kernel, out_rows, *arrays, scalars=None, scratch=()):
    specs = [in_vmem() for _ in arrays]
    operands = list(arrays)
    if scalars is not None:
        specs.append(in_smem())
        operands.append(scalars)
    return pl.pallas_call(
        kernel,
        in_specs=specs,
        out_specs=[in_vmem() for _ in out_rows],
        out_shape=rows_of(*out_rows),
        scratch_shapes=[pltpu.VMEM((count, LANES), F32) for count in scratch],
        compiler_params=pltpu.CompilerParams(vmem_limit_bytes=OWNER_VMEM_LIMIT),
    )(*operands)


def swap(message):
    devices = lax.axis_size("colblk") * lax.axis_size("rep")
    sent = message.reshape(devices, 1, message.shape[0] // devices * LANES)
    got = lax.all_to_all(sent, PLANE, 0, 0, tiled=True)
    return got.reshape(message.shape)


def from_all_planes(value):
    planes = lax.axis_size("rowblk")
    return [value] + [
        lax.ppermute(value, "rowblk", [(i, i ^ m) for i in range(planes)]) for m in (1, 3, 2)
    ]


def to_other_core(value):
    return lax.ppermute(value, "rep", [(0, 1), (1, 0)])


def along_ring(value, step):
    pairs = []
    for i in range(lax.axis_size("colblk")):
        base, z = i // RING * RING, i % RING
        pairs.append((i, base + (z + (step if z % 2 == 0 else -step)) % RING))
    return lax.ppermute(value, "colblk", pairs)


def across_rings(value, mask):
    pairs = [(i, i ^ (mask * RING)) for i in range(lax.axis_size("colblk"))]
    return lax.ppermute(value, "colblk", pairs)


def over_plane(value, pair):
    rows = value.shape[0] // 2
    is_first = lax.axis_index("rep") == 0
    low, high = value[:rows], value[rows:]
    mine = pair(jnp.where(is_first, low, high), to_other_core(jnp.where(is_first, high, low)))
    near, far = along_ring(mine, 1), along_ring(mine, -1)
    even = lax.axis_index("colblk") % 2 == 0
    above, below = jnp.where(even, near, far), jnp.where(even, far, near)
    two = pair(mine, below)
    three = pair(two, above)
    first = along_ring(jnp.where(even, three, two), 3)
    second = along_ring(jnp.where(even, two, three), -3)
    mine = pair(pair(three, first), second)
    mine = pair(
        pair(mine, across_rings(mine, 1)), pair(across_rings(mine, 3), across_rings(mine, 2))
    )
    return mine, to_other_core(mine)


def sum_and_peak(first, second):
    rows = lax.broadcasted_iota(jnp.int32, first.shape, 0)
    return jnp.where(rows < first.shape[0] // 2, first + second, jnp.maximum(first, second))


def on_device(
    tile_values,
    tile_rowpos,
    tile_owner,
    tile_colpos,
    cost_vector,
    upper_bound,
    primal_start,
    row_limits,
    sense_flags,
    dual_start,
    step_sizes,
):
    tiles, size = tile_values.shape[0], tile_values.shape[1]
    blocks = cost_vector.shape[0] // size
    devices = lax.axis_size("colblk") * lax.axis_size("rep")
    cost, upper, start, limits, senses, duals = (
        a.reshape(-1, LANES)
        for a in (cost_vector, upper_bound, primal_start, row_limits, sense_flags, dual_start)
    )
    rows = duals.shape[0]
    terms = [jax.ShapeDtypeStruct((tiles, size, size), BF16)] * 2

    peaks, columns, index, held = first_pass(
        jnp.concatenate([tile_rowpos, tile_owner[:, 0], tile_colpos]), tile_values, rows,
        lax.axis_size("colblk"),
    )
    message, high, low, row_scale = over_tiles(
        second_peaks_kernel, [index], [held, *over_plane(peaks, jnp.maximum), columns, duals],
        rows_of(7 * devices) + terms + rows_of(rows), [rows],
    )
    partial_sums, place = at_owner(
        functools.partial(first_owner_kernel, blocks), [3 * blocks, CAP * devices], swap(message)
    )
    message, primal_state = at_owner(
        functools.partial(first_primal_kernel, blocks), [4 * devices, 4 * blocks],
        *from_all_planes(partial_sums), place, cost, upper, start, scalars=step_sizes,
    )
    (image,) = over_tiles(
        functools.partial(forward_kernel, True), [index], [high, low, swap(message)],
        rows_of(2 * rows),
    )
    message, dual_state = over_tiles(
        transposed_kernel, [index, step_sizes],
        [high, low, *over_plane(image, sum_and_peak), row_scale, limits, senses, duals],
        rows_of(2 * devices, 3 * rows), [2 * rows, rows],
    )
    (partial_sums,) = at_owner(
        functools.partial(column_sum_kernel, blocks), [blocks], swap(message), place
    )
    message, primal = at_owner(
        second_primal_kernel, [2 * devices, blocks], *from_all_planes(partial_sums), place,
        primal_state, scalars=step_sizes,
    )
    (image,) = over_tiles(
        functools.partial(forward_kernel, False), [index], [high, low, swap(message)],
        rows_of(rows),
    )
    (dual_values,) = at_owner(
        last_dual_kernel, [rows], *over_plane(image, jnp.add), dual_state, limits, senses,
        scalars=step_sizes, scratch=[rows],
    )
    other = to_other_core(primal)
    is_first = lax.axis_index("rep") == 0
    halves = [jnp.where(is_first, primal, other), jnp.where(is_first, other, primal)]
    return jnp.stack(halves, axis=1).reshape(-1), dual_values.reshape(-1)


def solution(mesh):
    tiled = P(("rowblk", "colblk", "rep"))
    return jax.shard_map(
        on_device,
        mesh=mesh,
        in_specs=(
            P(("rowblk", "colblk", "rep"), None, None),
            tiled,
            P(("rowblk", "colblk", "rep"), None),
            tiled,
            P("colblk"),
            P("colblk"),
            P("colblk"),
            P("rowblk"),
            P("rowblk"),
            P("rowblk"),
            P(),
        ),
        out_specs=(P("colblk"), P("rowblk")),
        check_vma=False,
    )
```

```python
import functools

import jax
import jax.numpy as jnp
from jax import lax
from jax.experimental import pallas as pl
from jax.experimental.pallas import tpu as pltpu
from jax.sharding import PartitionSpec as P

FLOOR = 0.5
CAP = 2
LANES = 128
PLANE = ("colblk", "rep")
RING = 8
F32 = jnp.float32
BF16 = jnp.bfloat16
FIRST_VMEM_LIMIT = 53 * 1024 * 1024
TILE_VMEM_LIMIT = 20 * 1024 * 1024
OWNER_VMEM_LIMIT = 16 * 1024 * 1024
CHUNK = 2
SMALL = 2.0 ** -40
LARGE = 2.0 ** 40


def row_of(ref, index):
    return ref[pl.ds(index, 1), :]


def half(array, h):
    return array[:, h * LANES:(h + 1) * LANES]


def both_halves(low, high):
    return jnp.concatenate([low, high], axis=1)


def peak_over_lanes(magnitude):
    return jnp.max(jnp.maximum(half(magnitude, 0), half(magnitude, 1)).T, axis=0, keepdims=True)


def sum_over_lanes(products):
    return jnp.sum((half(products, 0) + half(products, 1)).T, axis=0, keepdims=True)


def down_the_rows(vector):
    parts = [jnp.broadcast_to(half(vector, h), (LANES, LANES)).T for h in range(2)]
    return jnp.concatenate(parts, axis=0)


def two_terms(vector):
    first = vector.astype(BF16).astype(F32)
    second = vector - first
    rows = lax.broadcasted_iota(jnp.int32, (16, vector.shape[1]), 0)
    stacked = jnp.where(rows == 0, first, jnp.where(rows == 1, second, 0.0))
    return stacked.astype(BF16)


def times(vector, high, low):
    left = two_terms(vector)
    total = jnp.dot(left, high, preferred_element_type=F32)
    total = total + jnp.dot(left, low, preferred_element_type=F32)
    return jnp.sum(total, axis=0, keepdims=True)


def inverse_root(peak):
    return 1.0 / jnp.sqrt(jnp.maximum(peak, FLOOR))


def places(index_ref, tile, tiles):
    row, owner, slot, position = (index_ref[n * tiles + tile] for n in range(4))
    return row, 2 * owner, slot, position


def join(out_ref, mine_ref, other_ref):
    core = lax.axis_index("rep")
    rows = mine_ref.shape[0] // 2
    for n in range(2):
        here = slice(n * rows, (n + 1) * rows)
        base = 2 * n * rows
        out_ref[pl.ds(pl.multiple_of(base + core * rows, 8), rows), :] = mine_ref[here, :]
        out_ref[pl.ds(pl.multiple_of(base + (1 - core) * rows, 8), rows), :] = other_ref[here, :]


def first_peaks_kernel(
    tiles, given_ref, tile_hbm, row_ref, column_ref, index_ref, tile_ref, used_ref, tile_sems
):
    def move(n):
        part = pl.ds(n * CHUNK, CHUNK)
        return pltpu.make_async_copy(tile_hbm.at[part], tile_ref.at[part], tile_sems.at[n])

    for n in range(tiles // CHUNK):
        move(n).start()
    row_ref[...] = jnp.zeros_like(row_ref)
    for owner in range(used_ref.shape[0]):
        used_ref[owner] = 0
    for tile in range(tiles):
        if tile % CHUNK == 0:
            move(tile // CHUNK).wait()
        row, owner, position = (given_ref[n * tiles + tile] for n in range(3))
        slot = used_ref[owner]
        used_ref[owner] = slot + 1
        for n, value in enumerate((row, owner, slot, position)):
            index_ref[n * tiles + tile] = value
        magnitude = jnp.abs(tile_ref[tile])
        column_ref[tile:tile + 1, :] = jnp.max(magnitude, axis=0, keepdims=True)
        rows = peak_over_lanes(magnitude)
        for h in range(2):
            at = row * 2 + h
            row_ref[pl.ds(at, 1), :] = jnp.maximum(row_of(row_ref, at), half(rows, h))


def second_peaks_kernel(
    tiles, index_ref, tile_ref, peak_ref, column_ref, dual_ref,
    out_ref, high_ref, low_ref, scale_ref, duals,
):
    scale_ref[...] = inverse_root(peak_ref[...])
    duals[...] = (dual_ref[...] / scale_ref[...]) * SMALL
    out_ref[...] = jnp.zeros_like(out_ref)
    upper = lax.broadcasted_iota(jnp.int32, (1, LANES), 1) >= LANES // 2
    for tile in range(tiles):
        row, owner, slot, position = places(index_ref, tile, tiles)
        down = down_the_rows(both_halves(*[row_of(scale_ref, row * 2 + h) for h in range(2)]))
        square = tile_ref[tile]
        scaled = both_halves(*[down * half(square, h) for h in range(2)])
        peaks = jnp.max(jnp.abs(scaled), axis=0, keepdims=True)
        high = scaled.astype(BF16)
        low = (scaled - high.astype(F32)).astype(BF16)
        high_ref[tile] = high
        low_ref[tile] = low
        sums = times(both_halves(*[row_of(duals, row * 2 + h) for h in range(2)]), high, low)
        before = column_ref[tile:tile + 1, :]
        for h in range(2):
            at = (owner + h) * 7
            for n, values in enumerate((before, peaks, sums)):
                out_ref[pl.ds(at + 2 * n + slot, 1), :] = half(values, h)
            out_ref[pl.ds(at + 6, 1), :] = jnp.where(
                upper == (slot == 1), position.astype(F32), row_of(out_ref, at + 6)
            )


def forward_kernel(with_peaks, tiles, index_ref, high_ref, low_ref, vector_ref, out_ref):
    each = 4 if with_peaks else 2
    part = out_ref.shape[0] // each
    out_ref[...] = jnp.zeros_like(out_ref)
    for tile in range(tiles):
        row, owner, slot, _ = places(index_ref, tile, tiles)
        at = [(owner + h) * each + slot for h in range(2)]
        entries = high_ref[tile].astype(F32) + low_ref[tile].astype(F32)
        vector = both_halves(*[row_of(vector_ref, a) for a in at])
        sums = sum_over_lanes(entries * vector)
        if with_peaks:
            scale = both_halves(*[row_of(vector_ref, a + 2) for a in at])
            peaks = peak_over_lanes(jnp.abs(entries * scale))
            start = row * 2 + jnp.where(row >= part // 2, part, 0)
        else:
            start = row * 2
        for h in range(2):
            to = start + h
            out_ref[pl.ds(to, 1), :] = row_of(out_ref, to) + half(sums, h)
            if with_peaks:
                to = to + part
                out_ref[pl.ds(to, 1), :] = jnp.maximum(row_of(out_ref, to), half(peaks, h))


def dual_step(before, factor, scale, image, limit_ref, sense_ref, step_ref):
    after = before + step_ref[0:1, 1:2] * (factor * image - scale * limit_ref[...])
    return jnp.where(sense_ref[...] == 1, jnp.maximum(after, 0.0), after)


def transposed_kernel(
    tiles, index_ref, high_ref, low_ref, mine_ref, other_ref, scale_ref, limit_ref,
    sense_ref, dual_ref, step_ref, out_ref, state_ref, joined, send,
):
    rows = dual_ref.shape[0]
    join(joined, mine_ref, other_ref)
    image = joined[0:rows, :]
    factor = inverse_root(joined[rows:2 * rows, :])
    scale = scale_ref[...] * factor
    after = dual_step(
        dual_ref[...] / scale, factor, scale, image, limit_ref, sense_ref, step_ref
    )
    for n, value in enumerate((factor, scale, after)):
        state_ref[n * rows:(n + 1) * rows, :] = value
    send[...] = (factor * SMALL) * after
    out_ref[...] = jnp.zeros_like(out_ref)
    for tile in range(tiles):
        row, owner, slot, _ = places(index_ref, tile, tiles)
        vector = both_halves(*[row_of(send, row * 2 + h) for h in range(2)])
        sums = times(vector, high_ref[tile], low_ref[tile])
        for h in range(2):
            out_ref[pl.ds((owner + h) * 2 + slot, 1), :] = half(sums, h)


def every(ref, offset, stride):
    return ref[pl.ds(offset, ref.shape[0] // stride, stride=stride), :]


def gathered_by_place(table, place):
    picked = jnp.zeros_like(place)
    for q in range(table.shape[0]):
        picked = jnp.where(place == q, table[q:q + 1, :], picked)
    return picked


def combined_by_place(entries, blocks, over, pair):
    out = []
    for q in range(blocks):
        parts = [
            over(jnp.where(place == q, value, 0.0), axis=0, keepdims=True)
            for value, place in entries
        ]
        out.append(functools.reduce(pair, parts))
    return jnp.concatenate(out, axis=0)


def peak_by_place(entries, blocks):
    return combined_by_place(entries, blocks, jnp.max, jnp.maximum)


def sum_by_place(entries, blocks):
    return combined_by_place(entries, blocks, jnp.sum, jnp.add)


def first_owner_kernel(blocks, got_ref, all_ref, place_ref):
    sources = got_ref.shape[0] // 7
    named = every(got_ref, 6, 7)
    slots = []
    for k in range(CAP):
        at = k * LANES // 2
        place = jnp.broadcast_to(named[:, at:at + 1], named.shape)
        place_ref[k * sources:(k + 1) * sources, :] = place
        slots.append(place)
    for n, by_place in enumerate((peak_by_place, peak_by_place, sum_by_place)):
        entries = [(every(got_ref, 2 * n + k, 7), slots[k]) for k in range(CAP)]
        all_ref[n * blocks:(n + 1) * blocks, :] = by_place(entries, blocks)


def own_columns(ref, blocks):
    first = ref[pl.ds(0, blocks, stride=2), :]
    second = ref[pl.ds(1, blocks, stride=2), :]
    return jnp.where(lax.axis_index("rep") == 0, first, second)


def first_primal_kernel(
    blocks, a0, a1, a2, a3, place_ref, cost_ref, upper_ref, start_ref, step_ref, out_ref, state_ref
):
    peaks = slice(0, 2 * blocks)
    peak = jnp.maximum(jnp.maximum(a0[peaks], a1[peaks]), jnp.maximum(a2[peaks], a3[peaks]))
    sums = (a0[2 * blocks:] + a1[2 * blocks:]) + (a2[2 * blocks:] + a3[2 * blocks:])
    first = inverse_root(peak[0:blocks])
    scale = first / jnp.sqrt(jnp.maximum(first * peak[blocks:], FLOOR))
    cost = scale * own_columns(cost_ref, blocks)
    upper = own_columns(upper_ref, blocks) / scale
    before = own_columns(start_ref, blocks) / scale
    after = jnp.clip(before - step_ref[0:1, 0:1] * (cost + (scale * LARGE) * sums), 0.0, upper)
    send = scale * (2.0 * after - before)
    for n, value in enumerate((scale, cost, upper, after)):
        state_ref[n * blocks:(n + 1) * blocks, :] = value
    sources = place_ref.shape[0] // CAP
    for k in range(CAP):
        place = place_ref[k * sources:(k + 1) * sources, :]
        out_ref[pl.ds(k, sources, stride=4), :] = gathered_by_place(send, place)
        out_ref[pl.ds(2 + k, sources, stride=4), :] = gathered_by_place(first, place)


def column_sum_kernel(blocks, got_ref, place_ref, out_ref):
    sources = got_ref.shape[0] // 2
    out_ref[...] = sum_by_place(
        [(every(got_ref, k, 2), place_ref[k * sources:(k + 1) * sources, :]) for k in range(CAP)],
        blocks,
    )


def second_primal_kernel(s0, s1, s2, s3, place_ref, state_ref, step_ref, out_ref, primal_ref):
    blocks = s0.shape[0]
    scale, cost, upper, before = (state_ref[n * blocks:(n + 1) * blocks, :] for n in range(4))
    sums = (s0[...] + s1[...]) + (s2[...] + s3[...])
    after = jnp.clip(before - step_ref[0:1, 0:1] * (cost + (scale * LARGE) * sums), 0.0, upper)
    send = scale * (2.0 * after - before)
    primal_ref[...] = scale * after
    sources = place_ref.shape[0] // CAP
    for k in range(CAP):
        place = place_ref[k * sources:(k + 1) * sources, :]
        out_ref[pl.ds(k, sources, stride=2), :] = gathered_by_place(send, place)


def last_dual_kernel(image_ref, state_ref, limit_ref, sense_ref, step_ref, out_ref):
    rows = limit_ref.shape[0]
    factor, scale, before = (state_ref[n * rows:(n + 1) * rows, :] for n in range(3))
    after = dual_step(before, factor, scale, image_ref[...], limit_ref, sense_ref, step_ref)
    out_ref[...] = scale * after


def in_vmem():
    return pl.BlockSpec(memory_space=pltpu.VMEM)


def in_smem():
    return pl.BlockSpec(memory_space=pltpu.SMEM)


def rows_of(*counts):
    return [jax.ShapeDtypeStruct((count, LANES), F32) for count in counts]


def over_tiles(kernel, index, arrays, out_shape, scratch=()):
    tiles = arrays[0].shape[0]
    return pl.pallas_call(
        functools.partial(kernel, tiles),
        in_specs=[in_smem()] + [in_vmem()] * len(arrays),
        out_specs=[in_vmem()] * len(out_shape),
        out_shape=out_shape,
        scratch_shapes=[pltpu.VMEM((count, LANES), F32) for count in scratch],
        compiler_params=pltpu.CompilerParams(vmem_limit_bytes=TILE_VMEM_LIMIT),
    )(index, *arrays)


def first_pass(given, tile_values, row_rows, owner_count):
    tiles, size = tile_values.shape[0], tile_values.shape[1]
    return pl.pallas_call(
        functools.partial(first_peaks_kernel, tiles),
        in_specs=[in_smem(), pl.BlockSpec(memory_space=pltpu.HBM)],
        out_specs=[in_vmem(), in_vmem(), in_smem()],
        out_shape=[
            jax.ShapeDtypeStruct((row_rows, LANES), F32),
            jax.ShapeDtypeStruct((tiles, size), F32),
            jax.ShapeDtypeStruct((4 * tiles,), jnp.int32),
        ],
        scratch_shapes=[
            pltpu.VMEM((tiles, size, size), F32),
            pltpu.SMEM((owner_count,), jnp.int32), pltpu.SemaphoreType.DMA((tiles // CHUNK,)),
        ],
        compiler_params=pltpu.CompilerParams(vmem_limit_bytes=FIRST_VMEM_LIMIT),
    )(given, tile_values)


def at_owner(kernel, out_rows, *arrays):
    return pl.pallas_call(
        kernel,
        in_specs=[in_vmem()] * len(arrays),
        out_specs=[in_vmem()] * len(out_rows),
        out_shape=rows_of(*out_rows),
        compiler_params=pltpu.CompilerParams(vmem_limit_bytes=OWNER_VMEM_LIMIT),
    )(*arrays)


def swap(message):
    devices = lax.axis_size("colblk") * lax.axis_size("rep")
    sent = message.reshape(devices, 1, message.shape[0] // devices * LANES)
    got = lax.all_to_all(sent, PLANE, 0, 0, tiled=True)
    return got.reshape(message.shape)


def from_all_planes(value):
    planes = lax.axis_size("rowblk")
    return [value] + [
        lax.ppermute(value, "rowblk", [(i, i ^ m) for i in range(planes)]) for m in (1, 3, 2)
    ]


def to_other_core(value):
    return lax.ppermute(value, "rep", [(0, 1), (1, 0)])


def along_ring(step):
    return lambda i: i // RING * RING + (i + (step if i % 2 == 0 else -step)) % RING


def across_rings(mask):
    return lambda i: i ^ (mask * RING)


def by_core(value, first, second=None):
    maps = (first, second or first)
    pairs = [
        (2 * i + core, 2 * maps[core](i) + core)
        for i in range(lax.axis_size("colblk")) for core in range(2)
    ]
    return lax.ppermute(value, PLANE, pairs)


def in_plane():
    return lax.axis_index("rep") == 0, lax.axis_index("colblk") % 2 == 0


def over_plane(value, pair):
    is_first, even = in_plane()
    rows = value.shape[0] // 2
    value = pair(value, to_other_core(value))
    came = by_core(value, along_ring(1), along_ring(-1))
    other = to_other_core(came)
    above = jnp.where(even == is_first, came, other)
    below = jnp.where(even == is_first, other, came)
    two = pair(value, below)
    three = pair(two, above)
    came = by_core(jnp.where(even == is_first, three, two), along_ring(3), along_ring(-3))
    value = pair(pair(three, came), to_other_core(came))
    came = by_core(value, across_rings(1), across_rings(3))
    opposite = by_core(jnp.where(is_first, value[:rows], value[rows:]), across_rings(2))
    low, high = came[:rows], came[rows:]
    came = jnp.concatenate(
        [
            jnp.where(is_first, pair(low, opposite), low),
            jnp.where(is_first, high, pair(high, opposite)),
        ],
        axis=0,
    )
    return pair(pair(value, came), to_other_core(came))


def over_plane_in_halves(value, pair):
    is_first, even = in_plane()
    rows = value.shape[0] // 2
    low, high = value[:rows], value[rows:]
    mine = pair(jnp.where(is_first, low, high), to_other_core(jnp.where(is_first, high, low)))
    near, far = by_core(mine, along_ring(1)), by_core(mine, along_ring(-1))
    above, below = jnp.where(even, near, far), jnp.where(even, far, near)
    two = pair(mine, below)
    three = pair(two, above)
    first = by_core(jnp.where(even, three, two), along_ring(3))
    second = by_core(jnp.where(even, two, three), along_ring(-3))
    mine = pair(pair(three, first), second)
    one, three, two = (by_core(mine, across_rings(mask)) for mask in (1, 3, 2))
    mine = pair(pair(mine, one), pair(three, two))
    return mine, to_other_core(mine)


def sum_and_peak(first, second):
    rows = lax.broadcasted_iota(jnp.int32, first.shape, 0)
    return jnp.where(rows < first.shape[0] // 2, first + second, jnp.maximum(first, second))


def on_device(
    tile_values,
    tile_rowpos,
    tile_owner,
    tile_colpos,
    cost_vector,
    upper_bound,
    primal_start,
    row_limits,
    sense_flags,
    dual_start,
    step_sizes,
):
    tiles, size = tile_values.shape[0], tile_values.shape[1]
    blocks = cost_vector.shape[0] // size
    devices = lax.axis_size("colblk") * lax.axis_size("rep")
    cost, upper, start, limits, senses, duals = (
        a.reshape(-1, LANES)
        for a in (cost_vector, upper_bound, primal_start, row_limits, sense_flags, dual_start)
    )
    rows = duals.shape[0]
    steps = step_sizes.reshape(1, 2)
    terms = [jax.ShapeDtypeStruct((tiles, size, size), BF16)] * 2

    peaks, columns, index = first_pass(
        jnp.concatenate([tile_rowpos, tile_owner[:, 0], tile_colpos]), tile_values, rows,
        lax.axis_size("colblk"),
    )
    message, high, low, row_scale = over_tiles(
        second_peaks_kernel, index, [tile_values, over_plane(peaks, jnp.maximum), columns, duals],
        rows_of(7 * devices) + terms + rows_of(rows), [rows],
    )
    partial_sums, place = at_owner(
        functools.partial(first_owner_kernel, blocks), [3 * blocks, CAP * devices], swap(message)
    )
    message, primal_state = at_owner(
        functools.partial(first_primal_kernel, blocks), [4 * devices, 4 * blocks],
        *from_all_planes(partial_sums), place, cost, upper, start, steps,
    )
    (image,) = over_tiles(
        functools.partial(forward_kernel, True), index, [high, low, swap(message)],
        rows_of(2 * rows),
    )
    message, dual_state = over_tiles(
        transposed_kernel, index,
        [high, low, *over_plane_in_halves(image, sum_and_peak), row_scale, limits, senses, duals, steps],
        rows_of(2 * devices, 3 * rows), [2 * rows, rows],
    )
    (partial_sums,) = at_owner(
        functools.partial(column_sum_kernel, blocks), [blocks], swap(message), place
    )
    message, primal = at_owner(
        second_primal_kernel, [2 * devices, blocks], *from_all_planes(partial_sums), place,
        primal_state, steps,
    )
    (image,) = over_tiles(
        functools.partial(forward_kernel, False), index, [high, low, swap(message)],
        rows_of(rows),
    )
    (dual_values,) = at_owner(
        last_dual_kernel, [rows], over_plane(image, jnp.add), dual_state, limits, senses, steps
    )
    other = to_other_core(primal)
    is_first = lax.axis_index("rep") == 0
    halves = [jnp.where(is_first, primal, other), jnp.where(is_first, other, primal)]
    return jnp.stack(halves, axis=1).reshape(-1), dual_values.reshape(-1)


def solution(mesh):
    tiled = P(("rowblk", "colblk", "rep"))
    return jax.shard_map(
        on_device,
        mesh=mesh,
        in_specs=(
            P(("rowblk", "colblk", "rep"), None, None),
            tiled,
            P(("rowblk", "colblk", "rep"), None),
            tiled,
            P("colblk"),
            P("colblk"),
            P("colblk"),
            P("rowblk"),
            P("rowblk"),
            P("rowblk"),
            P(),
        ),
        out_specs=(P("colblk"), P("rowblk")),
        check_vma=False,
    )
```

```python
import functools

import jax
import jax.numpy as jnp
from jax import lax
from jax.experimental import pallas as pl
from jax.experimental.pallas import tpu as pltpu
from jax.sharding import PartitionSpec as P

FLOOR = 0.5
CAP = 2
LANES = 128
PLANE = ("colblk", "rep")
RING = 8
F32 = jnp.float32
BF16 = jnp.bfloat16
FIRST_VMEM_LIMIT = 43 * 1024 * 1024
TILE_VMEM_LIMIT = 20 * 1024 * 1024
OWNER_VMEM_LIMIT = 16 * 1024 * 1024
CHUNK = 4
SMALL = 2.0 ** -59
LARGE = 2.0 ** 60


def row_of(ref, index):
    return ref[pl.ds(index, 1), :]


def half(array, h):
    return array[:, h * LANES:(h + 1) * LANES]


def both_halves(low, high):
    return jnp.concatenate([low, high], axis=1)


def peak_over_lanes(magnitude):
    return jnp.max(jnp.maximum(half(magnitude, 0), half(magnitude, 1)).T, axis=0, keepdims=True)


def sum_over_lanes(products):
    return jnp.sum((half(products, 0) + half(products, 1)).T, axis=0, keepdims=True)


def down_the_rows(vector):
    parts = [jnp.broadcast_to(half(vector, h), (LANES, LANES)).T for h in range(2)]
    return jnp.concatenate(parts, axis=0)


def two_terms(vector):
    first = vector.astype(BF16).astype(F32)
    second = vector - first
    rows = lax.broadcasted_iota(jnp.int32, (16, vector.shape[1]), 0)
    stacked = jnp.where(rows == 0, first, jnp.where(rows == 1, second, 0.0))
    return stacked.astype(BF16)


def times(vector, high, low):
    left = two_terms(vector)
    total = jnp.dot(left, high, preferred_element_type=F32)
    total = total + jnp.dot(left, low, preferred_element_type=F32)
    return jnp.sum(total, axis=0, keepdims=True)


def inverse_root(peak):
    return 1.0 / jnp.sqrt(jnp.maximum(peak, FLOOR))


def places(index_ref, tile, tiles):
    row, owner, slot, position = (index_ref[n * tiles + tile] for n in range(4))
    return row, 2 * owner, slot, position


def join(out_ref, mine_ref, other_ref):
    core = lax.axis_index("rep")
    rows = mine_ref.shape[0] // 2
    for n in range(2):
        here = slice(n * rows, (n + 1) * rows)
        base = 2 * n * rows
        out_ref[pl.ds(pl.multiple_of(base + core * rows, 8), rows), :] = mine_ref[here, :]
        out_ref[pl.ds(pl.multiple_of(base + (1 - core) * rows, 8), rows), :] = other_ref[here, :]


def first_peaks_kernel(
    tiles, given_any, tile_hbm, row_ref, column_ref, index_ref, high_ref, low_ref, flag_ref,
    tile_ref, given_ref, used_ref, tile_sems, given_sem,
):
    def move(n):
        part = pl.ds(n * CHUNK, CHUNK)
        return pltpu.make_async_copy(tile_hbm.at[part], tile_ref.at[part], tile_sems.at[n])

    for n in range(tiles // CHUNK):
        move(n).start()
    given = pltpu.make_async_copy(given_any, given_ref, given_sem)
    given.start()
    flags = (lax.axis_index("rep") == 0, lax.rem(lax.axis_index("colblk"), 2) == 0)
    for n, flag in enumerate(flags):
        flag_ref[n:n + 1, :] = jnp.zeros((1, LANES), F32) + jnp.where(flag, 1.0, 0.0)
    row_ref[...] = jnp.zeros_like(row_ref)
    for owner in range(used_ref.shape[0]):
        used_ref[owner] = 0
    given.wait()
    for tile in range(tiles):
        if tile % CHUNK == 0:
            move(tile // CHUNK).wait()
        row, owner, position = (given_ref[n * tiles + tile] for n in range(3))
        slot = used_ref[owner]
        used_ref[owner] = slot + 1
        for n, value in enumerate((row, owner, slot, position)):
            index_ref[n * tiles + tile] = value
        square = tile_ref[tile]
        halved = 0.5 * square
        high = halved.astype(BF16)
        high_ref[tile] = high
        low_ref[tile] = (halved - high.astype(F32)).astype(BF16)
        magnitude = jnp.abs(square)
        column_ref[tile:tile + 1, :] = jnp.max(magnitude, axis=0, keepdims=True)
        rows = peak_over_lanes(magnitude)
        for h in range(2):
            at = row * 2 + h
            row_ref[pl.ds(at, 1), :] = jnp.maximum(row_of(row_ref, at), half(rows, h))


def second_peaks_kernel(
    tiles, index_ref, high_ref, low_ref, peak_ref, column_ref, dual_ref, out_ref, scale_ref
):
    scale_ref[...] = inverse_root(peak_ref[...])
    out_ref[...] = jnp.zeros_like(out_ref)
    upper = lax.broadcasted_iota(jnp.int32, (1, LANES), 1) >= LANES // 2
    for tile in range(tiles):
        row, owner, slot, position = places(index_ref, tile, tiles)
        down = down_the_rows(both_halves(*[row_of(scale_ref, row * 2 + h) for h in range(2)]))
        high, low = high_ref[tile], low_ref[tile]
        entries = high.astype(F32) + low.astype(F32)
        scaled = both_halves(*[down * half(entries, h) for h in range(2)])
        peaks = 2.0 * jnp.max(jnp.abs(scaled), axis=0, keepdims=True)
        duals = both_halves(*[row_of(dual_ref, row * 2 + h) for h in range(2)])
        sums = times(SMALL * duals, high, low)
        before = column_ref[tile:tile + 1, :]
        for h in range(2):
            at = (owner + h) * 7
            for n, values in enumerate((before, peaks, sums)):
                out_ref[pl.ds(at + 2 * n + slot, 1), :] = half(values, h)
            out_ref[pl.ds(at + 6, 1), :] = jnp.where(
                upper == (slot == 1), position.astype(F32), row_of(out_ref, at + 6)
            )


def forward_kernel(with_peaks, tiles, index_ref, high_ref, low_ref, vector_ref, out_ref):
    each = 4 if with_peaks else 2
    part = out_ref.shape[0] // each
    out_ref[...] = jnp.zeros_like(out_ref)
    for tile in range(tiles):
        row, owner, slot, _ = places(index_ref, tile, tiles)
        at = [(owner + h) * each + slot for h in range(2)]
        entries = high_ref[tile].astype(F32) + low_ref[tile].astype(F32)
        vector = both_halves(*[row_of(vector_ref, a) for a in at])
        sums = sum_over_lanes(entries * vector)
        if with_peaks:
            scale = both_halves(*[row_of(vector_ref, a + 2) for a in at])
            peaks = peak_over_lanes(jnp.abs(entries * scale))
            start = row * 2 + jnp.where(row >= part // 2, part, 0)
        else:
            start = row * 2
        for h in range(2):
            to = start + h
            out_ref[pl.ds(to, 1), :] = row_of(out_ref, to) + half(sums, h)
            if with_peaks:
                to = to + part
                out_ref[pl.ds(to, 1), :] = jnp.maximum(row_of(out_ref, to), half(peaks, h))


def dual_step(before, scale, sums, limit_ref, sense_ref, step_ref):
    image = (LARGE * scale) * sums
    after = before + step_ref[0:1, 1:2] * (image - scale * limit_ref[...])
    return jnp.where(sense_ref[...] == 1, jnp.maximum(after, 0.0), after)


def transposed_kernel(
    tiles, index_ref, high_ref, low_ref, mine_ref, other_ref, scale_ref, limit_ref,
    sense_ref, dual_ref, step_ref, out_ref, state_ref, joined, send,
):
    rows = dual_ref.shape[0]
    join(joined, mine_ref, other_ref)
    scale = scale_ref[...]
    scale = scale * inverse_root(scale * (2.0 * joined[rows:2 * rows, :]))
    after = dual_step(
        dual_ref[...] / scale, scale, joined[0:rows, :], limit_ref, sense_ref, step_ref
    )
    for n, value in enumerate((scale, after)):
        state_ref[n * rows:(n + 1) * rows, :] = value
    send[...] = SMALL * (scale * after)
    out_ref[...] = jnp.zeros_like(out_ref)
    for tile in range(tiles):
        row, owner, slot, _ = places(index_ref, tile, tiles)
        vector = both_halves(*[row_of(send, row * 2 + h) for h in range(2)])
        sums = times(vector, high_ref[tile], low_ref[tile])
        for h in range(2):
            out_ref[pl.ds((owner + h) * 2 + slot, 1), :] = half(sums, h)


def every(ref, offset, stride):
    return ref[pl.ds(offset, ref.shape[0] // stride, stride=stride), :]


def gathered_by_place(table, place):
    picked = jnp.zeros_like(place)
    for q in range(table.shape[0]):
        picked = jnp.where(place == q, table[q:q + 1, :], picked)
    return picked


def combined_by_place(entries, blocks, over, pair):
    out = []
    for q in range(blocks):
        parts = [
            over(jnp.where(place == q, value, 0.0), axis=0, keepdims=True)
            for value, place in entries
        ]
        out.append(functools.reduce(pair, parts))
    return jnp.concatenate(out, axis=0)


def peak_by_place(entries, blocks):
    return combined_by_place(entries, blocks, jnp.max, jnp.maximum)


def sum_by_place(entries, blocks):
    return combined_by_place(entries, blocks, jnp.sum, jnp.add)


def first_owner_kernel(blocks, got_ref, all_ref, place_ref):
    sources = got_ref.shape[0] // 7
    named = every(got_ref, 6, 7)
    slots = []
    for k in range(CAP):
        at = k * LANES // 2
        place = jnp.broadcast_to(named[:, at:at + 1], named.shape)
        place_ref[k * sources:(k + 1) * sources, :] = place
        slots.append(place)
    for n, by_place in enumerate((peak_by_place, peak_by_place, sum_by_place)):
        entries = [(every(got_ref, 2 * n + k, 7), slots[k]) for k in range(CAP)]
        all_ref[n * blocks:(n + 1) * blocks, :] = by_place(entries, blocks)


def own_columns(ref, blocks):
    first = ref[pl.ds(0, blocks, stride=2), :]
    second = ref[pl.ds(1, blocks, stride=2), :]
    return jnp.where(lax.axis_index("rep") == 0, first, second)


def first_primal_kernel(
    blocks, a0, a1, a2, a3, place_ref, cost_ref, upper_ref, start_ref, step_ref, out_ref, state_ref
):
    peaks = slice(0, 2 * blocks)
    peak = jnp.maximum(jnp.maximum(a0[peaks], a1[peaks]), jnp.maximum(a2[peaks], a3[peaks]))
    sums = (a0[2 * blocks:] + a1[2 * blocks:]) + (a2[2 * blocks:] + a3[2 * blocks:])
    first = inverse_root(peak[0:blocks])
    scale = first / jnp.sqrt(jnp.maximum(first * peak[blocks:], FLOOR))
    cost = scale * own_columns(cost_ref, blocks)
    upper = own_columns(upper_ref, blocks) / scale
    before = own_columns(start_ref, blocks) / scale
    after = jnp.clip(before - step_ref[0:1, 0:1] * (cost + (LARGE * scale) * sums), 0.0, upper)
    send = SMALL * (scale * (2.0 * after - before))
    for n, value in enumerate((scale, cost, upper, after)):
        state_ref[n * blocks:(n + 1) * blocks, :] = value
    sources = place_ref.shape[0] // CAP
    for k in range(CAP):
        place = place_ref[k * sources:(k + 1) * sources, :]
        out_ref[pl.ds(k, sources, stride=4), :] = gathered_by_place(send, place)
        out_ref[pl.ds(2 + k, sources, stride=4), :] = gathered_by_place(first, place)


def column_sum_kernel(blocks, got_ref, place_ref, out_ref):
    sources = got_ref.shape[0] // 2
    out_ref[...] = sum_by_place(
        [(every(got_ref, k, 2), place_ref[k * sources:(k + 1) * sources, :]) for k in range(CAP)],
        blocks,
    )


def second_primal_kernel(s0, s1, s2, s3, place_ref, state_ref, step_ref, out_ref, primal_ref):
    blocks = s0.shape[0]
    scale, cost, upper, before = (state_ref[n * blocks:(n + 1) * blocks, :] for n in range(4))
    sums = (s0[...] + s1[...]) + (s2[...] + s3[...])
    after = jnp.clip(before - step_ref[0:1, 0:1] * (cost + (LARGE * scale) * sums), 0.0, upper)
    send = SMALL * (scale * (2.0 * after - before))
    primal_ref[...] = scale * after
    sources = place_ref.shape[0] // CAP
    for k in range(CAP):
        place = place_ref[k * sources:(k + 1) * sources, :]
        out_ref[pl.ds(k, sources, stride=2), :] = gathered_by_place(send, place)


def last_dual_kernel(image_ref, state_ref, limit_ref, sense_ref, step_ref, out_ref):
    rows = limit_ref.shape[0]
    scale, before = (state_ref[n * rows:(n + 1) * rows, :] for n in range(2))
    after = dual_step(before, scale, image_ref[...], limit_ref, sense_ref, step_ref)
    out_ref[...] = scale * after


def in_vmem():
    return pl.BlockSpec(memory_space=pltpu.VMEM)


def in_smem():
    return pl.BlockSpec(memory_space=pltpu.SMEM)


def rows_of(*counts):
    return [jax.ShapeDtypeStruct((count, LANES), F32) for count in counts]


def over_tiles(kernel, index, arrays, out_shape, scratch=()):
    tiles = arrays[0].shape[0]
    return pl.pallas_call(
        functools.partial(kernel, tiles),
        in_specs=[in_smem()] + [in_vmem()] * len(arrays),
        out_specs=[in_vmem()] * len(out_shape),
        out_shape=out_shape,
        scratch_shapes=[pltpu.VMEM((count, LANES), F32) for count in scratch],
        compiler_params=pltpu.CompilerParams(vmem_limit_bytes=TILE_VMEM_LIMIT),
    )(index, *arrays)


def first_pass(given, tile_values, row_rows, owner_count):
    tiles, size = tile_values.shape[0], tile_values.shape[1]
    return pl.pallas_call(
        functools.partial(first_peaks_kernel, tiles),
        in_specs=[pl.BlockSpec(memory_space=pl.ANY), pl.BlockSpec(memory_space=pltpu.HBM)],
        out_specs=[in_vmem(), in_vmem(), in_smem(), in_vmem(), in_vmem(), in_vmem()],
        out_shape=[
            jax.ShapeDtypeStruct((row_rows, LANES), F32),
            jax.ShapeDtypeStruct((tiles, size), F32),
            jax.ShapeDtypeStruct((4 * tiles,), jnp.int32),
            jax.ShapeDtypeStruct((tiles, size, size), BF16),
            jax.ShapeDtypeStruct((tiles, size, size), BF16),
            jax.ShapeDtypeStruct((2, LANES), F32),
        ],
        scratch_shapes=[
            pltpu.VMEM((tiles, size, size), F32),
            pltpu.SMEM((3 * tiles,), jnp.int32), pltpu.SMEM((owner_count,), jnp.int32),
            pltpu.SemaphoreType.DMA((tiles // CHUNK,)), pltpu.SemaphoreType.DMA,
        ],
        compiler_params=pltpu.CompilerParams(vmem_limit_bytes=FIRST_VMEM_LIMIT),
    )(given, tile_values)


def at_owner(kernel, out_rows, *arrays):
    return pl.pallas_call(
        kernel,
        in_specs=[in_vmem()] * len(arrays),
        out_specs=[in_vmem()] * len(out_rows),
        out_shape=rows_of(*out_rows),
        compiler_params=pltpu.CompilerParams(vmem_limit_bytes=OWNER_VMEM_LIMIT),
    )(*arrays)


def swap(message):
    devices = lax.axis_size("colblk") * lax.axis_size("rep")
    sent = message.reshape(devices, 1, message.shape[0] // devices * LANES)
    got = lax.all_to_all(sent, PLANE, 0, 0, tiled=True)
    return got.reshape(message.shape)


def from_all_planes(value):
    planes = lax.axis_size("rowblk")
    return [value] + [
        lax.ppermute(value, "rowblk", [(i, i ^ m) for i in range(planes)]) for m in (1, 3, 2)
    ]


def to_other_core(value):
    return lax.ppermute(value, "rep", [(0, 1), (1, 0)])


def along_ring(step):
    return lambda i: i // RING * RING + (i + (step if i % 2 == 0 else -step)) % RING


def across_rings(mask):
    return lambda i: i ^ (mask * RING)


def by_core(value, first, second=None):
    maps = (first, second or first)
    pairs = [
        (2 * i + core, 2 * maps[core](i) + core)
        for i in range(lax.axis_size("colblk")) for core in range(2)
    ]
    return lax.ppermute(value, PLANE, pairs)


def over_plane(value, pair, is_first, even):
    rows = value.shape[0] // 2
    value = pair(value, to_other_core(value))
    came = by_core(value, along_ring(1), along_ring(-1))
    other = to_other_core(came)
    above = jnp.where(even == is_first, came, other)
    below = jnp.where(even == is_first, other, came)
    two = pair(value, below)
    three = pair(two, above)
    came = by_core(jnp.where(even == is_first, three, two), along_ring(3), along_ring(-3))
    value = pair(pair(three, came), to_other_core(came))
    came = by_core(value, across_rings(1), across_rings(3))
    opposite = by_core(jnp.where(is_first, value[:rows], value[rows:]), across_rings(2))
    low, high = came[:rows], came[rows:]
    came = jnp.concatenate(
        [
            jnp.where(is_first, pair(low, opposite), low),
            jnp.where(is_first, high, pair(high, opposite)),
        ],
        axis=0,
    )
    return pair(pair(value, came), to_other_core(came))


def over_plane_in_halves(value, pair, is_first, even):
    rows = value.shape[0] // 2
    low, high = value[:rows], value[rows:]
    mine = pair(jnp.where(is_first, low, high), to_other_core(jnp.where(is_first, high, low)))
    near, far = by_core(mine, along_ring(1)), by_core(mine, along_ring(-1))
    above, below = jnp.where(even, near, far), jnp.where(even, far, near)
    two = pair(mine, below)
    three = pair(two, above)
    first = by_core(jnp.where(even, three, two), along_ring(3))
    second = by_core(jnp.where(even, two, three), along_ring(-3))
    mine = pair(pair(three, first), second)
    one, three, two = (by_core(mine, across_rings(mask)) for mask in (1, 3, 2))
    mine = pair(pair(mine, one), pair(three, two))
    return mine, to_other_core(mine)


def sum_and_peak(first, second):
    rows = lax.broadcasted_iota(jnp.int32, first.shape, 0)
    return jnp.where(rows < first.shape[0] // 2, first + second, jnp.maximum(first, second))


def on_device(
    tile_values,
    tile_rowpos,
    tile_owner,
    tile_colpos,
    cost_vector,
    upper_bound,
    primal_start,
    row_limits,
    sense_flags,
    dual_start,
    step_sizes,
):
    blocks = cost_vector.shape[0] // tile_values.shape[1]
    devices = lax.axis_size("colblk") * lax.axis_size("rep")
    cost, upper, start, limits, senses, duals = (
        a.reshape(-1, LANES)
        for a in (cost_vector, upper_bound, primal_start, row_limits, sense_flags, dual_start)
    )
    rows = duals.shape[0]
    steps = step_sizes.reshape(1, 2)

    peaks, columns, index, high, low, flags = first_pass(
        jnp.concatenate([tile_rowpos, tile_owner[:, 0], tile_colpos]), tile_values, rows,
        lax.axis_size("colblk"),
    )
    is_first, even = (flags[n:n + 1] > 0.5 for n in range(2))
    message, row_scale = over_tiles(
        second_peaks_kernel, index, [high, low, over_plane(peaks, jnp.maximum, is_first, even), columns, duals],
        rows_of(7 * devices, rows),
    )
    partial_sums, place = at_owner(
        functools.partial(first_owner_kernel, blocks), [3 * blocks, CAP * devices], swap(message)
    )
    message, primal_state = at_owner(
        functools.partial(first_primal_kernel, blocks), [4 * devices, 4 * blocks],
        *from_all_planes(partial_sums), place, cost, upper, start, steps,
    )
    (image,) = over_tiles(
        functools.partial(forward_kernel, True), index, [high, low, swap(message)],
        rows_of(2 * rows),
    )
    message, dual_state = over_tiles(
        transposed_kernel, index,
        [high, low, *over_plane_in_halves(image, sum_and_peak, is_first, even), row_scale, limits, senses, duals, steps],
        rows_of(2 * devices, 2 * rows), [2 * rows, rows],
    )
    (partial_sums,) = at_owner(
        functools.partial(column_sum_kernel, blocks), [blocks], swap(message), place
    )
    message, primal = at_owner(
        second_primal_kernel, [2 * devices, blocks], *from_all_planes(partial_sums), place,
        primal_state, steps,
    )
    (image,) = over_tiles(
        functools.partial(forward_kernel, False), index, [high, low, swap(message)],
        rows_of(rows),
    )
    (dual_values,) = at_owner(
        last_dual_kernel, [rows], over_plane(image, jnp.add, is_first, even), dual_state, limits, senses, steps
    )
    other = to_other_core(primal)
    halves = [jnp.where(is_first, primal, other), jnp.where(is_first, other, primal)]
    return jnp.stack(halves, axis=1).reshape(-1), dual_values.reshape(-1)


def solution(mesh):
    tiled = P(("rowblk", "colblk", "rep"))
    return jax.shard_map(
        on_device,
        mesh=mesh,
        in_specs=(
            P(("rowblk", "colblk", "rep"), None, None),
            tiled,
            P(("rowblk", "colblk", "rep"), None),
            tiled,
            P("colblk"),
            P("colblk"),
            P("colblk"),
            P("rowblk"),
            P("rowblk"),
            P("rowblk"),
            P(),
        ),
        out_specs=(P("colblk"), P("rowblk")),
        check_vma=False,
    )
```

```python
import functools

import jax
import jax.numpy as jnp
from jax import lax
from jax.experimental import pallas as pl
from jax.experimental.pallas import tpu as pltpu
from jax.sharding import PartitionSpec as P

FLOOR = 0.5
CAP = 2
LANES = 128
PLANE = ("colblk", "rep")
RING = 8
F32 = jnp.float32
BF16 = jnp.bfloat16
FIRST_VMEM_LIMIT = 34 * 1024 * 1024
TILE_VMEM_LIMIT = 20 * 1024 * 1024
OWNER_VMEM_LIMIT = 16 * 1024 * 1024
CHUNK = 4
SMALL = 2.0 ** -60
LARGE = 2.0 ** 60


def row_of(ref, index):
    return ref[pl.ds(index, 1), :]


def half(array, h):
    return array[:, h * LANES:(h + 1) * LANES]


def both_halves(low, high):
    return jnp.concatenate([low, high], axis=1)


def peak_over_lanes(magnitude):
    return jnp.max(jnp.maximum(half(magnitude, 0), half(magnitude, 1)).T, axis=0, keepdims=True)


def sum_over_lanes(products):
    return jnp.sum((half(products, 0) + half(products, 1)).T, axis=0, keepdims=True)


def down_the_rows(vector):
    parts = [jnp.broadcast_to(half(vector, h), (LANES, LANES)).T for h in range(2)]
    return jnp.concatenate(parts, axis=0)


def two_terms(vector):
    first = vector.astype(BF16).astype(F32)
    second = vector - first
    rows = lax.broadcasted_iota(jnp.int32, (16, vector.shape[1]), 0)
    stacked = jnp.where(rows == 0, first, jnp.where(rows == 1, second, 0.0))
    return stacked.astype(BF16)


def times(vector, high, low):
    left = two_terms(vector)
    total = jnp.dot(left, high, preferred_element_type=F32)
    total = total + jnp.dot(left, low, preferred_element_type=F32)
    return jnp.sum(total, axis=0, keepdims=True)


def inverse_root(peak):
    return 1.0 / jnp.sqrt(jnp.maximum(peak, FLOOR))


def places(index_ref, tile, tiles):
    row, owner, slot, position = (index_ref[n * tiles + tile] for n in range(4))
    return row, 2 * owner, slot, position


def join(out_ref, mine_ref, other_ref):
    core = lax.axis_index("rep")
    rows = mine_ref.shape[0] // 2
    for n in range(2):
        here = slice(n * rows, (n + 1) * rows)
        base = 2 * n * rows
        out_ref[pl.ds(pl.multiple_of(base + core * rows, 8), rows), :] = mine_ref[here, :]
        out_ref[pl.ds(pl.multiple_of(base + (1 - core) * rows, 8), rows), :] = other_ref[here, :]


def first_peaks_kernel(
    tiles, given_any, tile_hbm, row_ref, column_ref, index_ref, tile_ref, high_ref, low_ref,
    flag_ref, given_ref, used_ref, tile_sems, given_sem,
):
    def move(n):
        part = pl.ds(n * CHUNK, CHUNK)
        return pltpu.make_async_copy(tile_hbm.at[part], tile_ref.at[part], tile_sems.at[n])

    for n in range(tiles // CHUNK):
        move(n).start()
    given = pltpu.make_async_copy(given_any, given_ref, given_sem)
    given.start()
    flags = (lax.axis_index("rep") == 0, lax.rem(lax.axis_index("colblk"), 2) == 0)
    for n, flag in enumerate(flags):
        flag_ref[n:n + 1, :] = jnp.zeros((1, LANES), F32) + jnp.where(flag, 1.0, 0.0)
    row_ref[...] = jnp.zeros_like(row_ref)
    for owner in range(used_ref.shape[0]):
        used_ref[owner] = 0
    given.wait()
    for tile in range(tiles):
        if tile % CHUNK == 0:
            move(tile // CHUNK).wait()
        row, owner, position = (given_ref[n * tiles + tile] for n in range(3))
        slot = used_ref[owner]
        used_ref[owner] = slot + 1
        for n, value in enumerate((row, owner, slot, position)):
            index_ref[n * tiles + tile] = value
        square = tile_ref[tile]
        halved = 0.5 * square
        high = halved.astype(BF16)
        high_ref[tile] = high
        low_ref[tile] = (halved - high.astype(F32)).astype(BF16)
        magnitude = jnp.abs(square)
        column_ref[tile:tile + 1, :] = jnp.max(magnitude, axis=0, keepdims=True)
        rows = peak_over_lanes(magnitude)
        for h in range(2):
            at = row * 2 + h
            row_ref[pl.ds(at, 1), :] = jnp.maximum(row_of(row_ref, at), half(rows, h))


def first_sums_kernel(tiles, index_ref, high_ref, low_ref, dual_ref, sum_ref):
    for tile in range(tiles):
        row = index_ref[tile]
        duals = both_halves(*[row_of(dual_ref, row * 2 + h) for h in range(2)])
        sums = times((2.0 * SMALL) * duals, high_ref[tile], low_ref[tile])
        for h in range(2):
            sum_ref[h * tiles + tile:h * tiles + tile + 1, :] = half(sums, h)


def second_peaks_kernel(
    tiles, index_ref, tile_ref, peak_ref, column_ref, sum_ref, out_ref, scale_ref
):
    scale_ref[...] = inverse_root(peak_ref[...])
    out_ref[...] = jnp.zeros_like(out_ref)
    upper = lax.broadcasted_iota(jnp.int32, (1, LANES), 1) >= LANES // 2
    for tile in range(tiles):
        row, owner, slot, position = places(index_ref, tile, tiles)
        down = down_the_rows(both_halves(*[row_of(scale_ref, row * 2 + h) for h in range(2)]))
        square = jnp.abs(tile_ref[tile])
        peaks = [jnp.max(down * half(square, h), axis=0, keepdims=True) for h in range(2)]
        before = column_ref[tile:tile + 1, :]
        for h in range(2):
            at = (owner + h) * 7
            sums = sum_ref[h * tiles + tile:h * tiles + tile + 1, :]
            for n, values in enumerate((half(before, h), peaks[h], sums)):
                out_ref[pl.ds(at + 2 * n + slot, 1), :] = values
            out_ref[pl.ds(at + 6, 1), :] = jnp.where(
                upper == (slot == 1), position.astype(F32), row_of(out_ref, at + 6)
            )


def forward_kernel(with_peaks, tiles, index_ref, tile_ref, vector_ref, out_ref):
    each = 4 if with_peaks else 2
    part = out_ref.shape[0] // each
    out_ref[...] = jnp.zeros_like(out_ref)
    for tile in range(tiles):
        row, owner, slot, _ = places(index_ref, tile, tiles)
        at = [(owner + h) * each + slot for h in range(2)]
        entries = tile_ref[tile]
        vector = both_halves(*[row_of(vector_ref, a) for a in at])
        sums = sum_over_lanes(entries * vector)
        if with_peaks:
            scale = both_halves(*[row_of(vector_ref, a + 2) for a in at])
            peaks = peak_over_lanes(jnp.abs(entries * scale))
            start = row * 2 + jnp.where(row >= part // 2, part, 0)
        else:
            start = row * 2
        for h in range(2):
            to = start + h
            out_ref[pl.ds(to, 1), :] = row_of(out_ref, to) + half(sums, h)
            if with_peaks:
                to = to + part
                out_ref[pl.ds(to, 1), :] = jnp.maximum(row_of(out_ref, to), half(peaks, h))


def dual_step(before, scale, sums, limit_ref, sense_ref, step_ref):
    image = (LARGE * scale) * sums
    after = before + step_ref[0:1, 1:2] * (image - scale * limit_ref[...])
    return jnp.where(sense_ref[...] == 1, jnp.maximum(after, 0.0), after)


def transposed_kernel(
    tiles, index_ref, high_ref, low_ref, mine_ref, other_ref, scale_ref, limit_ref,
    sense_ref, dual_ref, step_ref, out_ref, state_ref, joined, send,
):
    rows = dual_ref.shape[0]
    join(joined, mine_ref, other_ref)
    scale = scale_ref[...]
    scale = scale * inverse_root(scale * joined[rows:2 * rows, :])
    after = dual_step(
        dual_ref[...] / scale, scale, joined[0:rows, :], limit_ref, sense_ref, step_ref
    )
    for n, value in enumerate((scale, after)):
        state_ref[n * rows:(n + 1) * rows, :] = value
    send[...] = (2.0 * SMALL) * (scale * after)
    out_ref[...] = jnp.zeros_like(out_ref)
    for tile in range(tiles):
        row, owner, slot, _ = places(index_ref, tile, tiles)
        vector = both_halves(*[row_of(send, row * 2 + h) for h in range(2)])
        sums = times(vector, high_ref[tile], low_ref[tile])
        for h in range(2):
            out_ref[pl.ds((owner + h) * 2 + slot, 1), :] = half(sums, h)


def every(ref, offset, stride):
    return ref[pl.ds(offset, ref.shape[0] // stride, stride=stride), :]


def gathered_by_place(table, place):
    picked = jnp.zeros_like(place)
    for q in range(table.shape[0]):
        picked = jnp.where(place == q, table[q:q + 1, :], picked)
    return picked


def combined_by_place(entries, blocks, over, pair):
    out = []
    for q in range(blocks):
        parts = [
            over(jnp.where(place == q, value, 0.0), axis=0, keepdims=True)
            for value, place in entries
        ]
        out.append(functools.reduce(pair, parts))
    return jnp.concatenate(out, axis=0)


def peak_by_place(entries, blocks):
    return combined_by_place(entries, blocks, jnp.max, jnp.maximum)


def sum_by_place(entries, blocks):
    return combined_by_place(entries, blocks, jnp.sum, jnp.add)


def first_owner_kernel(blocks, got_ref, all_ref, place_ref):
    sources = got_ref.shape[0] // 7
    named = every(got_ref, 6, 7)
    slots = []
    for k in range(CAP):
        at = k * LANES // 2
        place = jnp.broadcast_to(named[:, at:at + 1], named.shape)
        place_ref[k * sources:(k + 1) * sources, :] = place
        slots.append(place)
    for n, by_place in enumerate((peak_by_place, peak_by_place, sum_by_place)):
        entries = [(every(got_ref, 2 * n + k, 7), slots[k]) for k in range(CAP)]
        all_ref[n * blocks:(n + 1) * blocks, :] = by_place(entries, blocks)


def own_columns(ref, blocks):
    first = ref[pl.ds(0, blocks, stride=2), :]
    second = ref[pl.ds(1, blocks, stride=2), :]
    return jnp.where(lax.axis_index("rep") == 0, first, second)


def first_primal_kernel(
    blocks, a0, a1, a2, a3, place_ref, cost_ref, upper_ref, start_ref, step_ref, out_ref, state_ref
):
    peaks = slice(0, 2 * blocks)
    peak = jnp.maximum(jnp.maximum(a0[peaks], a1[peaks]), jnp.maximum(a2[peaks], a3[peaks]))
    sums = (a0[2 * blocks:] + a1[2 * blocks:]) + (a2[2 * blocks:] + a3[2 * blocks:])
    first = inverse_root(peak[0:blocks])
    scale = first / jnp.sqrt(jnp.maximum(first * peak[blocks:], FLOOR))
    cost = scale * own_columns(cost_ref, blocks)
    upper = own_columns(upper_ref, blocks) / scale
    before = own_columns(start_ref, blocks) / scale
    after = jnp.clip(before - step_ref[0:1, 0:1] * (cost + (LARGE * scale) * sums), 0.0, upper)
    send = SMALL * (scale * (2.0 * after - before))
    for n, value in enumerate((scale, cost, upper, after)):
        state_ref[n * blocks:(n + 1) * blocks, :] = value
    sources = place_ref.shape[0] // CAP
    for k in range(CAP):
        place = place_ref[k * sources:(k + 1) * sources, :]
        out_ref[pl.ds(k, sources, stride=4), :] = gathered_by_place(send, place)
        out_ref[pl.ds(2 + k, sources, stride=4), :] = gathered_by_place(first, place)


def column_sum_kernel(blocks, got_ref, place_ref, out_ref):
    sources = got_ref.shape[0] // 2
    out_ref[...] = sum_by_place(
        [(every(got_ref, k, 2), place_ref[k * sources:(k + 1) * sources, :]) for k in range(CAP)],
        blocks,
    )


def second_primal_kernel(s0, s1, s2, s3, place_ref, state_ref, step_ref, out_ref, primal_ref):
    blocks = s0.shape[0]
    scale, cost, upper, before = (state_ref[n * blocks:(n + 1) * blocks, :] for n in range(4))
    sums = (s0[...] + s1[...]) + (s2[...] + s3[...])
    after = jnp.clip(before - step_ref[0:1, 0:1] * (cost + (LARGE * scale) * sums), 0.0, upper)
    send = SMALL * (scale * (2.0 * after - before))
    primal_ref[...] = scale * after
    sources = place_ref.shape[0] // CAP
    for k in range(CAP):
        place = place_ref[k * sources:(k + 1) * sources, :]
        out_ref[pl.ds(k, sources, stride=2), :] = gathered_by_place(send, place)


def last_dual_kernel(image_ref, state_ref, limit_ref, sense_ref, step_ref, out_ref):
    rows = limit_ref.shape[0]
    scale, before = (state_ref[n * rows:(n + 1) * rows, :] for n in range(2))
    after = dual_step(before, scale, image_ref[...], limit_ref, sense_ref, step_ref)
    out_ref[...] = scale * after


def in_vmem():
    return pl.BlockSpec(memory_space=pltpu.VMEM)


def in_smem():
    return pl.BlockSpec(memory_space=pltpu.SMEM)


def rows_of(*counts):
    return [jax.ShapeDtypeStruct((count, LANES), F32) for count in counts]


def over_tiles(kernel, index, arrays, out_shape, scratch=()):
    tiles = arrays[0].shape[0]
    return pl.pallas_call(
        functools.partial(kernel, tiles),
        in_specs=[in_smem()] + [in_vmem()] * len(arrays),
        out_specs=[in_vmem()] * len(out_shape),
        out_shape=out_shape,
        scratch_shapes=[pltpu.VMEM((count, LANES), F32) for count in scratch],
        compiler_params=pltpu.CompilerParams(vmem_limit_bytes=TILE_VMEM_LIMIT),
    )(index, *arrays)


def first_pass(given, tile_values, row_rows, owner_count):
    tiles, size = tile_values.shape[0], tile_values.shape[1]
    return pl.pallas_call(
        functools.partial(first_peaks_kernel, tiles),
        in_specs=[pl.BlockSpec(memory_space=pl.ANY), pl.BlockSpec(memory_space=pltpu.HBM)],
        out_specs=[in_vmem(), in_vmem(), in_smem()] + [in_vmem()] * 4,
        out_shape=[
            jax.ShapeDtypeStruct((row_rows, LANES), F32),
            jax.ShapeDtypeStruct((tiles, size), F32),
            jax.ShapeDtypeStruct((4 * tiles,), jnp.int32),
            jax.ShapeDtypeStruct((tiles, size, size), F32),
            jax.ShapeDtypeStruct((tiles, size, size), BF16),
            jax.ShapeDtypeStruct((tiles, size, size), BF16),
            jax.ShapeDtypeStruct((2, LANES), F32),
        ],
        scratch_shapes=[
            pltpu.SMEM((3 * tiles,), jnp.int32), pltpu.SMEM((owner_count,), jnp.int32),
            pltpu.SemaphoreType.DMA((tiles // CHUNK,)), pltpu.SemaphoreType.DMA,
        ],
        compiler_params=pltpu.CompilerParams(vmem_limit_bytes=FIRST_VMEM_LIMIT),
    )(given, tile_values)


def at_owner(kernel, out_rows, *arrays):
    return pl.pallas_call(
        kernel,
        in_specs=[in_vmem()] * len(arrays),
        out_specs=[in_vmem()] * len(out_rows),
        out_shape=rows_of(*out_rows),
        compiler_params=pltpu.CompilerParams(vmem_limit_bytes=OWNER_VMEM_LIMIT),
    )(*arrays)


def swap(message):
    devices = lax.axis_size("colblk") * lax.axis_size("rep")
    sent = message.reshape(devices, 1, message.shape[0] // devices * LANES)
    got = lax.all_to_all(sent, PLANE, 0, 0, tiled=True)
    return got.reshape(message.shape)


def from_all_planes(value):
    planes = lax.axis_size("rowblk")
    return [value] + [
        lax.ppermute(value, "rowblk", [(i, i ^ m) for i in range(planes)]) for m in (1, 3, 2)
    ]


def to_other_core(value):
    return lax.ppermute(value, "rep", [(0, 1), (1, 0)])


def along_ring(step):
    return lambda i: i // RING * RING + (i + (step if i % 2 == 0 else -step)) % RING


def across_rings(mask):
    return lambda i: i ^ (mask * RING)


def by_core(value, first, second=None):
    maps = (first, second or first)
    pairs = [
        (2 * i + core, 2 * maps[core](i) + core)
        for i in range(lax.axis_size("colblk")) for core in range(2)
    ]
    return lax.ppermute(value, PLANE, pairs)


def over_plane(value, pair, is_first, even, beside=None):
    rows = value.shape[0] // 2
    value = pair(value, to_other_core(value))
    came = by_core(value, along_ring(1), along_ring(-1))
    other = to_other_core(came)
    above = jnp.where(even == is_first, came, other)
    below = jnp.where(even == is_first, other, came)
    two = pair(value, below)
    three = pair(two, above)
    came = by_core(jnp.where(even == is_first, three, two), along_ring(3), along_ring(-3))
    if beside is not None:
        came, beside = lax.optimization_barrier((came, beside))
    value = pair(pair(three, came), to_other_core(came))
    came = by_core(value, across_rings(1), across_rings(3))
    opposite = by_core(jnp.where(is_first, value[:rows], value[rows:]), across_rings(2))
    low, high = came[:rows], came[rows:]
    came = jnp.concatenate(
        [
            jnp.where(is_first, pair(low, opposite), low),
            jnp.where(is_first, high, pair(high, opposite)),
        ],
        axis=0,
    )
    value = pair(pair(value, came), to_other_core(came))
    return value if beside is None else (value, beside)


def over_plane_in_halves(value, pair, is_first, even):
    rows = value.shape[0] // 2
    low, high = value[:rows], value[rows:]
    mine = pair(jnp.where(is_first, low, high), to_other_core(jnp.where(is_first, high, low)))
    near, far = by_core(mine, along_ring(1)), by_core(mine, along_ring(-1))
    above, below = jnp.where(even, near, far), jnp.where(even, far, near)
    two = pair(mine, below)
    three = pair(two, above)
    first = by_core(jnp.where(even, three, two), along_ring(3))
    second = by_core(jnp.where(even, two, three), along_ring(-3))
    mine = pair(pair(three, first), second)
    one, three, two = (by_core(mine, across_rings(mask)) for mask in (1, 3, 2))
    mine = pair(pair(mine, one), pair(three, two))
    return mine, to_other_core(mine)


def sum_and_peak(first, second):
    rows = lax.broadcasted_iota(jnp.int32, first.shape, 0)
    return jnp.where(rows < first.shape[0] // 2, first + second, jnp.maximum(first, second))


def on_device(
    tile_values,
    tile_rowpos,
    tile_owner,
    tile_colpos,
    cost_vector,
    upper_bound,
    primal_start,
    row_limits,
    sense_flags,
    dual_start,
    step_sizes,
):
    blocks = cost_vector.shape[0] // tile_values.shape[1]
    devices = lax.axis_size("colblk") * lax.axis_size("rep")
    cost, upper, start, limits, senses, duals = (
        a.reshape(-1, LANES)
        for a in (cost_vector, upper_bound, primal_start, row_limits, sense_flags, dual_start)
    )
    rows = duals.shape[0]
    steps = step_sizes.reshape(1, 2)

    peaks, columns, index, held, high, low, flags = first_pass(
        jnp.concatenate([tile_rowpos, tile_owner[:, 0], tile_colpos]), tile_values, rows,
        lax.axis_size("colblk"),
    )
    is_first, even = (flags[n:n + 1] > 0.5 for n in range(2))
    (first_sums,) = over_tiles(
        first_sums_kernel, index, [high, low, duals],
        rows_of(2 * tile_values.shape[0]),
    )
    peaks, first_sums = over_plane(peaks, jnp.maximum, is_first, even, first_sums)
    message, row_scale = over_tiles(
        second_peaks_kernel, index, [held, peaks, columns, first_sums],
        rows_of(7 * devices, rows),
    )
    partial_sums, place = at_owner(
        functools.partial(first_owner_kernel, blocks), [3 * blocks, CAP * devices], swap(message)
    )
    message, primal_state = at_owner(
        functools.partial(first_primal_kernel, blocks), [4 * devices, 4 * blocks],
        *from_all_planes(partial_sums), place, cost, upper, start, steps,
    )
    (image,) = over_tiles(
        functools.partial(forward_kernel, True), index, [held, swap(message)],
        rows_of(2 * rows),
    )
    message, dual_state = over_tiles(
        transposed_kernel, index,
        [high, low, *over_plane_in_halves(image, sum_and_peak, is_first, even), row_scale, limits, senses, duals, steps],
        rows_of(2 * devices, 2 * rows), [2 * rows, rows],
    )
    (partial_sums,) = at_owner(
        functools.partial(column_sum_kernel, blocks), [blocks], swap(message), place
    )
    message, primal = at_owner(
        second_primal_kernel, [2 * devices, blocks], *from_all_planes(partial_sums), place,
        primal_state, steps,
    )
    (image,) = over_tiles(
        functools.partial(forward_kernel, False), index, [held, swap(message)],
        rows_of(rows),
    )
    (dual_values,) = at_owner(
        last_dual_kernel, [rows], over_plane(image, jnp.add, is_first, even), dual_state, limits, senses, steps
    )
    other = to_other_core(primal)
    halves = [jnp.where(is_first, primal, other), jnp.where(is_first, other, primal)]
    return jnp.stack(halves, axis=1).reshape(-1), dual_values.reshape(-1)


def solution(mesh):
    tiled = P(("rowblk", "colblk", "rep"))
    return jax.shard_map(
        on_device,
        mesh=mesh,
        in_specs=(
            P(("rowblk", "colblk", "rep"), None, None),
            tiled,
            P(("rowblk", "colblk", "rep"), None),
            tiled,
            P("colblk"),
            P("colblk"),
            P("colblk"),
            P("rowblk"),
            P("rowblk"),
            P("rowblk"),
            P(),
        ),
        out_specs=(P("colblk"), P("rowblk")),
        check_vma=False,
    )
```

```python
import functools

import jax
import jax.numpy as jnp
from jax import lax
from jax.experimental import pallas as pl
from jax.experimental.pallas import tpu as pltpu
from jax.sharding import PartitionSpec as P

FLOOR = 0.5
CAP = 2
LANES = 128
PLANE = ("colblk", "rep")
RING = 8
F32 = jnp.float32
BF16 = jnp.bfloat16
FIRST_VMEM_LIMIT = 42 * 1024 * 1024
TILE_VMEM_LIMIT = 20 * 1024 * 1024
OWNER_VMEM_LIMIT = 16 * 1024 * 1024
CHUNK = 4
DUAL_DOWN, DUAL_UP = 2.0 ** -40, 2.0 ** 40
PRIMAL_DOWN, PRIMAL_UP = 2.0 ** -30, 2.0 ** 30


def row_of(ref, index):
    return ref[pl.ds(index, 1), :]


def half(array, h):
    return array[:, h * LANES:(h + 1) * LANES]


def both_halves(low, high):
    return jnp.concatenate([low, high], axis=1)


def peak_over_lanes(magnitude):
    return jnp.max(jnp.maximum(half(magnitude, 0), half(magnitude, 1)).T, axis=0, keepdims=True)


def sum_over_lanes(products):
    return jnp.sum((half(products, 0) + half(products, 1)).T, axis=0, keepdims=True)


def down_the_rows(vector):
    parts = [jnp.broadcast_to(half(vector, h), (LANES, LANES)).T for h in range(2)]
    return jnp.concatenate(parts, axis=0)


def two_terms(vector):
    first = vector.astype(BF16).astype(F32)
    second = vector - first
    rows = lax.broadcasted_iota(jnp.int32, (16, vector.shape[1]), 0)
    stacked = jnp.where(rows == 0, first, jnp.where(rows == 1, second, 0.0))
    return stacked.astype(BF16)


def times(vector, high, low):
    left = two_terms(vector)
    total = jnp.dot(left, high, preferred_element_type=F32)
    total = total + jnp.dot(left, low, preferred_element_type=F32)
    return jnp.sum(total, axis=0, keepdims=True)


def inverse_root(peak):
    return 1.0 / jnp.sqrt(jnp.maximum(peak, FLOOR))


def places(index_ref, tile, tiles):
    row, owner, slot, position = (index_ref[n * tiles + tile] for n in range(4))
    return row, 2 * owner, slot, position


def join(out_ref, mine_ref, other_ref):
    core = lax.axis_index("rep")
    rows = mine_ref.shape[0] // 2
    for n in range(2):
        here = slice(n * rows, (n + 1) * rows)
        base = 2 * n * rows
        out_ref[pl.ds(pl.multiple_of(base + core * rows, 8), rows), :] = mine_ref[here, :]
        out_ref[pl.ds(pl.multiple_of(base + (1 - core) * rows, 8), rows), :] = other_ref[here, :]


def first_peaks_kernel(
    tiles, given_any, tile_hbm, row_ref, column_ref, index_ref, tile_ref, flag_ref,
    given_ref, used_ref, tile_sems, given_sem,
):
    def move(n):
        part = pl.ds(n * CHUNK, CHUNK)
        return pltpu.make_async_copy(tile_hbm.at[part], tile_ref.at[part], tile_sems.at[n])

    for n in range(tiles // CHUNK):
        move(n).start()
    given = pltpu.make_async_copy(given_any, given_ref, given_sem)
    given.start()
    flags = (lax.axis_index("rep") == 0, lax.rem(lax.axis_index("colblk"), 2) == 0)
    for n, flag in enumerate(flags):
        flag_ref[n:n + 1, :] = jnp.zeros((1, LANES), F32) + jnp.where(flag, 1.0, 0.0)
    row_ref[...] = jnp.zeros_like(row_ref)
    for owner in range(used_ref.shape[0]):
        used_ref[owner] = 0
    given.wait()
    for tile in range(tiles):
        if tile % CHUNK == 0:
            move(tile // CHUNK).wait()
        row, owner, position = (given_ref[n * tiles + tile] for n in range(3))
        slot = used_ref[owner]
        used_ref[owner] = slot + 1
        for n, value in enumerate((row, owner, slot, position)):
            index_ref[n * tiles + tile] = value
        magnitude = jnp.abs(tile_ref[tile])
        column_ref[tile:tile + 1, :] = jnp.max(magnitude, axis=0, keepdims=True)
        rows = peak_over_lanes(magnitude)
        for h in range(2):
            at = row * 2 + h
            row_ref[pl.ds(at, 1), :] = jnp.maximum(row_of(row_ref, at), half(rows, h))


def second_peaks_kernel(
    tiles, index_ref, tile_ref, peak_ref, column_ref, dual_ref,
    out_ref, high_ref, low_ref, scale_ref, duals,
):
    scale_ref[...] = inverse_root(peak_ref[...])
    duals[...] = (dual_ref[...] / scale_ref[...]) * DUAL_DOWN
    out_ref[...] = jnp.zeros_like(out_ref)
    upper = lax.broadcasted_iota(jnp.int32, (1, LANES), 1) >= LANES // 2
    for tile in range(tiles):
        row, owner, slot, position = places(index_ref, tile, tiles)
        down = down_the_rows(both_halves(*[row_of(scale_ref, row * 2 + h) for h in range(2)]))
        square = tile_ref[tile]
        scaled = both_halves(*[down * half(square, h) for h in range(2)])
        peaks = jnp.max(jnp.abs(scaled), axis=0, keepdims=True)
        high = scaled.astype(BF16)
        low = (scaled - high.astype(F32)).astype(BF16)
        high_ref[tile] = high
        low_ref[tile] = low
        sums = times(both_halves(*[row_of(duals, row * 2 + h) for h in range(2)]), high, low)
        before = column_ref[tile:tile + 1, :]
        for h in range(2):
            at = (owner + h) * 7
            for n, values in enumerate((before, peaks, sums)):
                out_ref[pl.ds(at + 2 * n + slot, 1), :] = half(values, h)
            out_ref[pl.ds(at + 6, 1), :] = jnp.where(
                upper == (slot == 1), position.astype(F32), row_of(out_ref, at + 6)
            )


def forward_kernel(with_peaks, tiles, index_ref, tile_ref, scale_ref, vector_ref, out_ref):
    each = 4 if with_peaks else 2
    part = out_ref.shape[0] // each
    out_ref[...] = jnp.zeros_like(out_ref)
    for tile in range(tiles):
        row, owner, slot, _ = places(index_ref, tile, tiles)
        scale = both_halves(*[row_of(scale_ref, (owner + h) * 4 + 2 + slot) for h in range(2)])
        vector = both_halves(*[row_of(vector_ref, (owner + h) * each + slot) for h in range(2)])
        scaled = tile_ref[tile] * scale
        sums = sum_over_lanes(scaled * vector)
        if with_peaks:
            peaks = peak_over_lanes(jnp.abs(scaled))
            start = row * 2 + jnp.where(row >= part // 2, part, 0)
        else:
            start = row * 2
        for h in range(2):
            to = start + h
            out_ref[pl.ds(to, 1), :] = row_of(out_ref, to) + half(sums, h)
            if with_peaks:
                to = to + part
                out_ref[pl.ds(to, 1), :] = jnp.maximum(row_of(out_ref, to), half(peaks, h))


def dual_step(before, scale, sums, limit_ref, sense_ref, step_ref):
    image = (PRIMAL_UP * scale) * sums
    after = before + step_ref[0:1, 1:2] * (image - scale * limit_ref[...])
    return jnp.where(sense_ref[...] == 1, jnp.maximum(after, 0.0), after)


def transposed_kernel(
    tiles, index_ref, high_ref, low_ref, mine_ref, other_ref, scale_ref, limit_ref,
    sense_ref, dual_ref, step_ref, out_ref, state_ref, joined, send,
):
    rows = dual_ref.shape[0]
    join(joined, mine_ref, other_ref)
    scale = scale_ref[...]
    factor = inverse_root(scale * joined[rows:2 * rows, :])
    scale = scale * factor
    after = dual_step(
        dual_ref[...] / scale, scale, joined[0:rows, :], limit_ref, sense_ref, step_ref
    )
    for n, value in enumerate((scale, after)):
        state_ref[n * rows:(n + 1) * rows, :] = value
    send[...] = (DUAL_DOWN * factor) * after
    out_ref[...] = jnp.zeros_like(out_ref)
    for tile in range(tiles):
        row, owner, slot, _ = places(index_ref, tile, tiles)
        vector = both_halves(*[row_of(send, row * 2 + h) for h in range(2)])
        sums = times(vector, high_ref[tile], low_ref[tile])
        for h in range(2):
            out_ref[pl.ds((owner + h) * 2 + slot, 1), :] = half(sums, h)


def every(ref, offset, stride):
    return ref[pl.ds(offset, ref.shape[0] // stride, stride=stride), :]


def gathered_by_place(table, place):
    picked = jnp.zeros_like(place)
    for q in range(table.shape[0]):
        picked = jnp.where(place == q, table[q:q + 1, :], picked)
    return picked


def combined_by_place(entries, blocks, over, pair):
    out = []
    for q in range(blocks):
        parts = [
            over(jnp.where(place == q, value, 0.0), axis=0, keepdims=True)
            for value, place in entries
        ]
        out.append(functools.reduce(pair, parts))
    return jnp.concatenate(out, axis=0)


def peak_by_place(entries, blocks):
    return combined_by_place(entries, blocks, jnp.max, jnp.maximum)


def sum_by_place(entries, blocks):
    return combined_by_place(entries, blocks, jnp.sum, jnp.add)


def first_owner_kernel(blocks, got_ref, all_ref, place_ref):
    sources = got_ref.shape[0] // 7
    named = every(got_ref, 6, 7)
    slots = []
    for k in range(CAP):
        at = k * LANES // 2
        place = jnp.broadcast_to(named[:, at:at + 1], named.shape)
        place_ref[k * sources:(k + 1) * sources, :] = place
        slots.append(place)
    for n, by_place in enumerate((peak_by_place, peak_by_place, sum_by_place)):
        entries = [(every(got_ref, 2 * n + k, 7), slots[k]) for k in range(CAP)]
        all_ref[n * blocks:(n + 1) * blocks, :] = by_place(entries, blocks)


def own_columns(ref, blocks):
    first = ref[pl.ds(0, blocks, stride=2), :]
    second = ref[pl.ds(1, blocks, stride=2), :]
    return jnp.where(lax.axis_index("rep") == 0, first, second)


def first_primal_kernel(
    blocks, a0, a1, a2, a3, place_ref, cost_ref, upper_ref, start_ref, step_ref, out_ref, state_ref
):
    peaks = slice(0, 2 * blocks)
    peak = jnp.maximum(jnp.maximum(a0[peaks], a1[peaks]), jnp.maximum(a2[peaks], a3[peaks]))
    sums = (a0[2 * blocks:] + a1[2 * blocks:]) + (a2[2 * blocks:] + a3[2 * blocks:])
    first = inverse_root(peak[0:blocks])
    factor = inverse_root(first * peak[blocks:])
    scale = first * factor
    cost = scale * own_columns(cost_ref, blocks)
    upper = own_columns(upper_ref, blocks) / scale
    before = own_columns(start_ref, blocks) / scale
    after = jnp.clip(before - step_ref[0:1, 0:1] * (cost + (DUAL_UP * scale) * sums), 0.0, upper)
    send = (PRIMAL_DOWN * factor) * (2.0 * after - before)
    for n, value in enumerate((factor, scale, cost, upper, after)):
        state_ref[n * blocks:(n + 1) * blocks, :] = value
    sources = place_ref.shape[0] // CAP
    for k in range(CAP):
        place = place_ref[k * sources:(k + 1) * sources, :]
        out_ref[pl.ds(k, sources, stride=4), :] = gathered_by_place(send, place)
        out_ref[pl.ds(2 + k, sources, stride=4), :] = gathered_by_place(first, place)


def column_sum_kernel(blocks, got_ref, place_ref, out_ref):
    sources = got_ref.shape[0] // 2
    out_ref[...] = sum_by_place(
        [(every(got_ref, k, 2), place_ref[k * sources:(k + 1) * sources, :]) for k in range(CAP)],
        blocks,
    )


def second_primal_kernel(s0, s1, s2, s3, place_ref, state_ref, step_ref, out_ref, primal_ref):
    blocks = s0.shape[0]
    factor, scale, cost, upper, before = (
        state_ref[n * blocks:(n + 1) * blocks, :] for n in range(5)
    )
    sums = (s0[...] + s1[...]) + (s2[...] + s3[...])
    after = jnp.clip(before - step_ref[0:1, 0:1] * (cost + (DUAL_UP * scale) * sums), 0.0, upper)
    send = (PRIMAL_DOWN * factor) * (2.0 * after - before)
    primal_ref[...] = scale * after
    sources = place_ref.shape[0] // CAP
    for k in range(CAP):
        place = place_ref[k * sources:(k + 1) * sources, :]
        out_ref[pl.ds(k, sources, stride=2), :] = gathered_by_place(send, place)


def last_dual_kernel(image_ref, state_ref, limit_ref, sense_ref, step_ref, out_ref):
    rows = limit_ref.shape[0]
    scale, before = (state_ref[n * rows:(n + 1) * rows, :] for n in range(2))
    after = dual_step(before, scale, image_ref[...], limit_ref, sense_ref, step_ref)
    out_ref[...] = scale * after


def in_vmem():
    return pl.BlockSpec(memory_space=pltpu.VMEM)


def in_smem():
    return pl.BlockSpec(memory_space=pltpu.SMEM)


def rows_of(*counts):
    return [jax.ShapeDtypeStruct((count, LANES), F32) for count in counts]


def over_tiles(kernel, index, arrays, out_shape, scratch=()):
    tiles = arrays[0].shape[0]
    return pl.pallas_call(
        functools.partial(kernel, tiles),
        in_specs=[in_smem()] + [in_vmem()] * len(arrays),
        out_specs=[in_vmem()] * len(out_shape),
        out_shape=out_shape,
        scratch_shapes=[pltpu.VMEM((count, LANES), F32) for count in scratch],
        compiler_params=pltpu.CompilerParams(vmem_limit_bytes=TILE_VMEM_LIMIT),
    )(index, *arrays)


def first_pass(given, tile_values, row_rows, owner_count):
    tiles, size = tile_values.shape[0], tile_values.shape[1]
    return pl.pallas_call(
        functools.partial(first_peaks_kernel, tiles),
        in_specs=[pl.BlockSpec(memory_space=pl.ANY), pl.BlockSpec(memory_space=pltpu.HBM)],
        out_specs=[in_vmem(), in_vmem(), in_smem()] + [in_vmem()] * 2,
        out_shape=[
            jax.ShapeDtypeStruct((row_rows, LANES), F32),
            jax.ShapeDtypeStruct((tiles, size), F32),
            jax.ShapeDtypeStruct((4 * tiles,), jnp.int32),
            jax.ShapeDtypeStruct((tiles, size, size), F32),
            jax.ShapeDtypeStruct((2, LANES), F32),
        ],
        scratch_shapes=[
            pltpu.SMEM((3 * tiles,), jnp.int32), pltpu.SMEM((owner_count,), jnp.int32),
            pltpu.SemaphoreType.DMA((tiles // CHUNK,)), pltpu.SemaphoreType.DMA,
        ],
        compiler_params=pltpu.CompilerParams(vmem_limit_bytes=FIRST_VMEM_LIMIT),
    )(given, tile_values)


def at_owner(kernel, out_rows, *arrays):
    return pl.pallas_call(
        kernel,
        in_specs=[in_vmem()] * len(arrays),
        out_specs=[in_vmem()] * len(out_rows),
        out_shape=rows_of(*out_rows),
        compiler_params=pltpu.CompilerParams(vmem_limit_bytes=OWNER_VMEM_LIMIT),
    )(*arrays)


def swap(message):
    devices = lax.axis_size("colblk") * lax.axis_size("rep")
    sent = message.reshape(devices, 1, message.shape[0] // devices * LANES)
    got = lax.all_to_all(sent, PLANE, 0, 0, tiled=True)
    return got.reshape(message.shape)


def from_all_planes(value):
    planes = lax.axis_size("rowblk")
    return [value] + [
        lax.ppermute(value, "rowblk", [(i, i ^ m) for i in range(planes)]) for m in (1, 3, 2)
    ]


def to_other_core(value):
    return lax.ppermute(value, "rep", [(0, 1), (1, 0)])


def along_ring(step):
    return lambda i: i // RING * RING + (i + (step if i % 2 == 0 else -step)) % RING


def across_rings(mask):
    return lambda i: i ^ (mask * RING)


def by_core(value, first, second=None):
    maps = (first, second or first)
    pairs = [
        (2 * i + core, 2 * maps[core](i) + core)
        for i in range(lax.axis_size("colblk")) for core in range(2)
    ]
    return lax.ppermute(value, PLANE, pairs)


def over_plane(value, pair, is_first, even):
    rows = value.shape[0] // 2
    value = pair(value, to_other_core(value))
    came = by_core(value, along_ring(1), along_ring(-1))
    other = to_other_core(came)
    above = jnp.where(even == is_first, came, other)
    below = jnp.where(even == is_first, other, came)
    two = pair(value, below)
    three = pair(two, above)
    came = by_core(jnp.where(even == is_first, three, two), along_ring(3), along_ring(-3))
    value = pair(pair(three, came), to_other_core(came))
    came = by_core(value, across_rings(1), across_rings(3))
    opposite = by_core(jnp.where(is_first, value[:rows], value[rows:]), across_rings(2))
    low, high = came[:rows], came[rows:]
    came = jnp.concatenate(
        [
            jnp.where(is_first, pair(low, opposite), low),
            jnp.where(is_first, high, pair(high, opposite)),
        ],
        axis=0,
    )
    return pair(pair(value, came), to_other_core(came))


def over_plane_in_halves(value, pair, is_first, even):
    rows = value.shape[0] // 2
    low, high = value[:rows], value[rows:]
    mine = pair(jnp.where(is_first, low, high), to_other_core(jnp.where(is_first, high, low)))
    near, far = by_core(mine, along_ring(1)), by_core(mine, along_ring(-1))
    above, below = jnp.where(even, near, far), jnp.where(even, far, near)
    two = pair(mine, below)
    three = pair(two, above)
    first = by_core(jnp.where(even, three, two), along_ring(3))
    second = by_core(jnp.where(even, two, three), along_ring(-3))
    mine = pair(pair(three, first), second)
    one, three, two = (by_core(mine, across_rings(mask)) for mask in (1, 3, 2))
    mine = pair(pair(mine, one), pair(three, two))
    return mine, to_other_core(mine)


def sum_and_peak(first, second):
    rows = lax.broadcasted_iota(jnp.int32, first.shape, 0)
    return jnp.where(rows < first.shape[0] // 2, first + second, jnp.maximum(first, second))


def on_device(
    tile_values,
    tile_rowpos,
    tile_owner,
    tile_colpos,
    cost_vector,
    upper_bound,
    primal_start,
    row_limits,
    sense_flags,
    dual_start,
    step_sizes,
):
    blocks = cost_vector.shape[0] // tile_values.shape[1]
    devices = lax.axis_size("colblk") * lax.axis_size("rep")
    cost, upper, start, limits, senses, duals = (
        a.reshape(-1, LANES)
        for a in (cost_vector, upper_bound, primal_start, row_limits, sense_flags, dual_start)
    )
    rows = duals.shape[0]
    steps = step_sizes.reshape(1, 2)
    terms = [jax.ShapeDtypeStruct(tile_values.shape, BF16)] * 2

    peaks, columns, index, held, flags = first_pass(
        jnp.concatenate([tile_rowpos, tile_owner[:, 0], tile_colpos]), tile_values, rows,
        lax.axis_size("colblk"),
    )
    is_first, even = (flags[n:n + 1] > 0.5 for n in range(2))
    message, high, low, row_scale = over_tiles(
        second_peaks_kernel, index,
        [held, over_plane(peaks, jnp.maximum, is_first, even), columns, duals],
        rows_of(7 * devices) + terms + rows_of(rows), [rows],
    )
    partial_sums, place = at_owner(
        functools.partial(first_owner_kernel, blocks), [3 * blocks, CAP * devices], swap(message)
    )
    message, primal_state = at_owner(
        functools.partial(first_primal_kernel, blocks), [4 * devices, 5 * blocks],
        *from_all_planes(partial_sums), place, cost, upper, start, steps,
    )
    scales = swap(message)
    (image,) = over_tiles(
        functools.partial(forward_kernel, True), index, [held, scales, scales],
        rows_of(2 * rows),
    )
    message, dual_state = over_tiles(
        transposed_kernel, index,
        [high, low, *over_plane_in_halves(image, sum_and_peak, is_first, even), row_scale, limits, senses, duals, steps],
        rows_of(2 * devices, 2 * rows), [2 * rows, rows],
    )
    (partial_sums,) = at_owner(
        functools.partial(column_sum_kernel, blocks), [blocks], swap(message), place
    )
    message, primal = at_owner(
        second_primal_kernel, [2 * devices, blocks], *from_all_planes(partial_sums), place,
        primal_state, steps,
    )
    (image,) = over_tiles(
        functools.partial(forward_kernel, False), index, [held, scales, swap(message)],
        rows_of(rows),
    )
    (dual_values,) = at_owner(
        last_dual_kernel, [rows], over_plane(image, jnp.add, is_first, even), dual_state, limits, senses, steps
    )
    other = to_other_core(primal)
    halves = [jnp.where(is_first, primal, other), jnp.where(is_first, other, primal)]
    return jnp.stack(halves, axis=1).reshape(-1), dual_values.reshape(-1)


def solution(mesh):
    tiled = P(("rowblk", "colblk", "rep"))
    return jax.shard_map(
        on_device,
        mesh=mesh,
        in_specs=(
            P(("rowblk", "colblk", "rep"), None, None),
            tiled,
            P(("rowblk", "colblk", "rep"), None),
            tiled,
            P("colblk"),
            P("colblk"),
            P("colblk"),
            P("rowblk"),
            P("rowblk"),
            P("rowblk"),
            P(),
        ),
        out_specs=(P("colblk"), P("rowblk")),
        check_vma=False,
    )
```
